32 devices in a mesh: section: 2 (over core), ctx: 16 (over z, y, x).
Axes of the slice: x: 2, y: 2, z: 4, core: 2. Of those that a mesh axis runs over, the one named last changes fastest.
Arguments:
- queries: bfloat16 [2, 4096, 1024], P('section', 'ctx'), may hold values from -6 to 6
- keys: bfloat16 [2, 4096, 128], P('section', 'ctx'), may hold values from -6 to 6
- values: bfloat16 [2, 4096, 128], P('section', 'ctx'), may hold values from -6 to 6
- attn_out: bfloat16 [2, 4096, 1024], P('section', 'ctx'), may hold values from -3 to 3
- log_sums: float32 [2, 8, 4096], P('section', None, 'ctx'), may hold values from 2 to 6
- grad_held: bfloat16 [2, 4096, 1024], P('section', 'ctx'), may hold values from -6 to 6
- doc_ids: int32 [4096], P('ctx'), may hold values from 0 to 15, never falling along the last dimension, each value on 1 to 512 neighbouring positions
Outputs:
- grad_queries: bfloat16 [2, 4096, 1024], P('section', 'ctx')
- grad_keys: bfloat16 [2, 4096, 128], P('section', 'ctx')
- grad_values: bfloat16 [2, 4096, 128], P('section', 'ctx')
The draws below stay inside these ranges and needn't reach their ends.
Inputs may be any that keep to these rules, and one draw needn't show every extreme that they name: `doc_ids`: document numbers never fall along the sequence; every document spans at most 512 positions and one spans exactly 512.
All inputs are finite; a program needn't handle non-finite values.
Results may differ from the reference program's by a relative error of at most 0.0049.
Values may be sent and summed in bfloat16 or wider, within the bound.
No kernel may reach another device: no remote copies, remote signals or barrier semaphores. Data moves between devices by JAX's collectives and lax.ppermute only.
A program may use at most 64 MiB of HBM per device.

```python
import math
import jax
import jax.numpy as jnp
import numpy as np
from jax import lax

HD = 128
HQ = 8
TOK_DEV = 256
HOPS = 2
DOC_MOST = 512
SEQ = 4096
N_SECTION = 2
N_CTX = 16


def level_of(own_key, shape, cuts, least, high):
    factor_of = 1.0
    for axis_at, blocks in cuts:
        draws = jax.random.uniform(jax.random.fold_in(jax.random.fold_in(own_key, 6), axis_at), (blocks,), jnp.float32, least / len(cuts), high / len(cuts))
        factor_of = factor_of * jnp.repeat(jnp.exp(draws), shape[axis_at] // blocks).reshape((-1,) + (1,) * (len(shape) - 1 - axis_at))
    return factor_of


def split_up(amount, total, most, slope):
    weights = [(1 << 20) // math.isqrt(grade ** slope) + 1 for grade in range(2, amount + 1)]
    surplus, holding = total - most - (amount - 1), [1] * (amount - 1)
    while surplus > 0:
        movable = [i for i in range(amount - 1) if holding[i] < most]
        whole, budget = sum([weights[i] for i in movable]), surplus
        for i in movable:
            extra = min(most - holding[i], max(1, budget * weights[i] // whole), surplus)
            holding[i] = holding[i] + extra
            surplus = surplus - extra
    return np.array([most] + holding)


def uneven_parts(stream_key, number_of, total, reach, slope):
    if number_of == 2:
        one = jax.random.randint(stream_key, (), max(1, total - reach), min(reach, total - 1) + 1)
        return jnp.stack([one, total - one])
    sizes = jnp.asarray(split_up(number_of, total, reach, slope), jnp.int32)
    twos = (number_of - 1) // 2
    source_of, taker = sizes[1:1 + 2 * twos:2], sizes[2:2 + 2 * twos:2]
    room = jnp.minimum(source_of - 1, reach - taker)
    shifted = jax.random.randint(jax.random.fold_in(stream_key, 1), (twos,), 0, 1 << 20) % (room + 1)
    sizes = sizes.at[1:1 + 2 * twos:2].set(source_of - shifted).at[2:2 + 2 * twos:2].set(taker + shifted)
    return sizes[jax.random.permutation(jax.random.fold_in(stream_key, 2), number_of)]


def bell_draw(rng, dims, deviation, bound, pieces=(), kind=jnp.bfloat16):
    level = level_of(rng, dims, pieces, -0.22, 0.18) if pieces else 1.0
    values = jax.random.normal(rng, dims, jnp.float32) * deviation * level
    return jnp.minimum(jnp.maximum(values, -bound), bound).astype(kind)


def setup_inputs(seed: int = 0) -> dict:
    arg_keys = jax.random.split(jax.random.key(seed), 8)
    return {
        "queries": bell_draw(arg_keys[0], (N_SECTION, SEQ, HQ * HD), 1.0, 6.0, ((0, 2), (1, 16))),
        "keys": bell_draw(arg_keys[1], (N_SECTION, SEQ, HD), 1.0, 6.0, ((0, 2), (1, 16))),
        "values": bell_draw(arg_keys[2], (N_SECTION, SEQ, HD), 1.0, 6.0, ((0, 2), (1, 16))),
        "attn_out": bell_draw(arg_keys[3], (N_SECTION, SEQ, HQ * HD), 0.5, 3.0, ((0, 2), (1, 16))),
        "log_sums": jnp.clip(2.0 + 4.0 * jax.random.uniform(arg_keys[4], (N_SECTION, HQ, SEQ), jnp.float32) ** level_of(arg_keys[4], (N_SECTION, HQ, SEQ), ((0, 2), (2, 16)), -0.2, 0.2), 2.0, 6.0),
        "grad_held": bell_draw(arg_keys[5], (N_SECTION, SEQ, HQ * HD), 1.0, 6.0, ((0, 2), (1, 16))),
        "doc_ids": jnp.searchsorted(jnp.cumsum(uneven_parts(arg_keys[6], N_CTX, SEQ, DOC_MOST, 1)), jnp.arange(SEQ), side="right").astype(jnp.int32),
    }


def block_grads(query_block, out_block, grad_block, lse_block, query_docs, query_pos, key_window, value_window, key_docs, key_pos):
    row_count = query_block.shape[0]
    head_count = lse_block.shape[0]
    head_width = key_window.shape[1]
    score_scale = float(head_width) ** -0.5
    q_heads = query_block.astype(jnp.float32).reshape(row_count, head_count, head_width)
    out_heads = out_block.astype(jnp.float32).reshape(row_count, head_count, head_width)
    grad_heads = grad_block.astype(jnp.float32).reshape(row_count, head_count, head_width)
    key_float = key_window.astype(jnp.float32)
    value_float = value_window.astype(jnp.float32)
    deltas = jnp.einsum('qhd,qhd->hq', grad_heads, out_heads)
    scores = jnp.einsum('qhd,kd->hqk', q_heads, key_float) * score_scale
    allowed = (query_docs[:, None] == key_docs[None, :]) & (key_pos[None, :] <= query_pos[:, None]) & (key_pos[None, :] >= 0)
    weights = jnp.where(allowed[None], jnp.exp(scores - lse_block[:, :, None]), jnp.float32(0.0))
    weights_low = weights.astype(jnp.bfloat16).astype(jnp.float32)
    weight_grads = jnp.einsum('qhd,kd->hqk', grad_heads, value_float)
    score_grads = (weights * (weight_grads - deltas[:, :, None])).astype(jnp.bfloat16).astype(jnp.float32)
    grad_q = jnp.einsum('hqk,kd->qhd', score_grads, key_float) * score_scale
    grad_k = jnp.einsum('hqk,qhd->kd', score_grads, q_heads) * score_scale
    grad_v = jnp.einsum('hqk,qhd->kd', weights_low, grad_heads)
    return grad_q.reshape(row_count, head_count * head_width), grad_k, grad_v


def section_grads(queries, keys, values, attn_out, log_sums, arrived, doc_ids):
    sequence = queries.shape[0]
    margin = HOPS * TOK_DEV
    head_width = keys.shape[1]
    window_rows = margin + TOK_DEV
    keys_padded = jnp.concatenate([jnp.zeros((margin, head_width), keys.dtype), keys], axis=0)
    values_padded = jnp.concatenate([jnp.zeros((margin, head_width), values.dtype), values], axis=0)
    docs_padded = jnp.concatenate([jnp.full((margin,), -1, jnp.int32), doc_ids.astype(jnp.int32)], axis=0)
    pos_padded = jnp.arange(sequence + margin, dtype=jnp.int32) - margin

    def advance(accumulated, block_index):
        grad_keys, grad_values = accumulated
        block_start = (block_index * TOK_DEV).astype(jnp.int32)
        query_pos = block_start + jnp.arange(TOK_DEV, dtype=jnp.int32)
        grad_q, grad_k, grad_v = block_grads(
            lax.dynamic_slice_in_dim(queries, block_start, TOK_DEV, 0),
            lax.dynamic_slice_in_dim(attn_out, block_start, TOK_DEV, 0),
            lax.dynamic_slice_in_dim(arrived, block_start, TOK_DEV, 0),
            lax.dynamic_slice_in_dim(log_sums, block_start, TOK_DEV, 1),
            lax.dynamic_slice_in_dim(doc_ids.astype(jnp.int32), block_start, TOK_DEV, 0),
            query_pos,
            lax.dynamic_slice_in_dim(keys_padded, block_start, window_rows, 0),
            lax.dynamic_slice_in_dim(values_padded, block_start, window_rows, 0),
            lax.dynamic_slice_in_dim(docs_padded, block_start, window_rows, 0),
            lax.dynamic_slice_in_dim(pos_padded, block_start, window_rows, 0))
        grad_keys = lax.dynamic_update_slice_in_dim(grad_keys, lax.dynamic_slice_in_dim(grad_keys, block_start, window_rows, 0) + grad_k, block_start, 0)
        grad_values = lax.dynamic_update_slice_in_dim(grad_values, lax.dynamic_slice_in_dim(grad_values, block_start, window_rows, 0) + grad_v, block_start, 0)
        return (grad_keys, grad_values), grad_q.astype(jnp.bfloat16)

    zeros_start = jnp.zeros((sequence + margin, head_width), jnp.float32)
    (grad_keys, grad_values), grad_blocks = lax.scan(advance, (zeros_start, zeros_start), jnp.arange(sequence // TOK_DEV, dtype=jnp.int32))
    grad_queries = grad_blocks.reshape(sequence, queries.shape[1])
    return grad_queries, grad_keys[margin:].astype(jnp.bfloat16), grad_values[margin:].astype(jnp.bfloat16)


def reference(queries, keys, values, attn_out, log_sums, grad_held, doc_ids):
    results = [section_grads(queries[section_index], keys[section_index], values[section_index], attn_out[section_index], log_sums[section_index], grad_held[(section_index + 1) % N_SECTION], doc_ids) for section_index in range(N_SECTION)]
    grad_queries = jnp.stack([entry[0] for entry in results])
    grad_keys = jnp.stack([entry[1] for entry in results])
    grad_values = jnp.stack([entry[2] for entry in results])
    return (grad_queries, grad_keys, grad_values)
```

```python
import functools

import jax
import jax.numpy as jnp
from jax import lax
from jax.experimental import pallas as pl
from jax.experimental.pallas import tpu as pltpu
from jax.sharding import PartitionSpec as P

HOPS = 2
DOC_ROWS = 16
LOG2_E = 1.4426950408889634
MASKED = -1e30

F32 = jnp.float32
BF16 = jnp.bfloat16


def from_behind(block, axis, distance):
    devices = range(lax.axis_size(axis))
    route = [((i - distance) % len(devices), i) for i in devices]
    return lax.ppermute(block, axis, route)


def shifted(array, axis, by):
    devices = lax.axis_size(axis)
    pairs = [(i, i + by) for i in range(devices) if 0 <= i + by < devices]
    return lax.ppermute(array, axis, pairs)


def dot_nt(a, b):
    return lax.dot_general(a, b, (((1,), (1,)), ((), ())), preferred_element_type=F32)


def dot_nn(a, b):
    return lax.dot_general(a, b, (((1,), (0,)), ((), ())), preferred_element_type=F32)


def vmem(count):
    return [pl.BlockSpec(memory_space=pltpu.VMEM)] * count


def pack_kernel(keys, values, docs, packed):
    rows, width = keys.shape[1:]
    packed[0:rows, 0:width] = keys[0]
    packed[0:rows, width : 2 * width] = values[0]
    docs_row = docs[...].astype(F32).astype(BF16)
    packed[rows : rows + DOC_ROWS, :] = jnp.broadcast_to(docs_row, (DOC_ROWS, docs_row.shape[1]))


def grads_kernel(place, queries, attn_out, grads, log_sums, docs, own, near, far, dq, own_sums, near_sums, far_sums, bias):
    rows = queries.shape[1]
    heads = log_sums.shape[1]
    width = queries.shape[2] // heads
    scale = float(width) ** -0.5
    blocks = (own, near, far)
    shard = place[0]

    docs_row = docs[...].astype(F32)
    docs_col = jnp.transpose(jnp.broadcast_to(docs_row, (width, rows)))
    docs_col = jnp.concatenate([docs_col] * (rows // width), axis=1)
    key_at = lax.broadcasted_iota(jnp.int32, (rows, rows), 0)
    query_at = lax.broadcasted_iota(jnp.int32, (rows, rows), 1)
    bias[0] = jnp.where((docs_col == docs_row) & (key_at <= query_at), 0.0, MASKED)
    for hop in range(1, HOPS + 1):
        far_docs = blocks[hop][rows : rows + DOC_ROWS, :].astype(F32)[0:1]
        far_col = jnp.transpose(jnp.broadcast_to(far_docs, (width, rows)))
        far_col = jnp.concatenate([far_col] * (rows // width), axis=1)
        bias[hop] = jnp.where((far_col == docs_row) & (shard >= hop), 0.0, MASKED)

    sums_k = [None] * (HOPS + 1)
    sums_v = [None] * (HOPS + 1)
    keys_turned = [jnp.transpose(block[0:rows, 0:width].astype(F32)).astype(BF16) for block in blocks]
    one = jnp.ones((8, width), BF16)
    for head in range(heads):
        part = slice(head * width, (head + 1) * width)
        q = queries[0, :, part]
        g = grads[0, :, part]
        product = g.astype(F32) * attn_out[0, :, part].astype(F32)
        high = product.astype(BF16)
        low = (product - high.astype(F32)).astype(BF16)
        delta = (dot_nt(one, high) + dot_nt(one, low))[0:1]
        lse = log_sums[0, head : head + 1, :] * LOG2_E
        dq_turned = None
        for hop in range(HOPS + 1):
            block = blocks[hop]
            scores = dot_nt(block[0:rows, 0:width], q)
            weights = jnp.exp2(scores * (scale * LOG2_E) - lse + bias[hop])
            weight_grads = dot_nt(block[0:rows, width : 2 * width], g)
            score_grads = (weights * (weight_grads - delta)).astype(BF16)
            term_v = dot_nn(weights.astype(BF16), g)
            term_k = dot_nn(score_grads, q)
            term_q = dot_nn(keys_turned[hop], score_grads)
            sums_v[hop] = term_v if head == 0 else sums_v[hop] + term_v
            sums_k[hop] = term_k if head == 0 else sums_k[hop] + term_k
            dq_turned = term_q if hop == 0 else dq_turned + term_q
        dq[0, :, part] = jnp.transpose(dq_turned * scale).astype(BF16)
    for hop, out in enumerate((own_sums, near_sums, far_sums)):
        out[:, 0:width] = (sums_k[hop] * scale).astype(out.dtype)
        out[:, width : 2 * width] = sums_v[hop].astype(out.dtype)


def add_kernel(own_sums, near_sums, far_sums, grad_keys, grad_values):
    width = grad_keys.shape[2]
    total = own_sums[...] + near_sums[...].astype(F32) + far_sums[...].astype(F32)
    grad_keys[0] = total[:, 0:width].astype(BF16)
    grad_values[0] = total[:, width : 2 * width].astype(BF16)


def per_device(queries, keys, values, attn_out, log_sums, grad_held, doc_ids):
    arrived = from_behind(grad_held, "section", -1)
    rows, width = keys.shape[1:]
    docs = doc_ids.reshape(1, rows)
    packed = pl.pallas_call(
        pack_kernel,
        out_shape=jax.ShapeDtypeStruct((rows + DOC_ROWS, 2 * width), BF16),
        in_specs=vmem(3),
        out_specs=pl.BlockSpec(memory_space=pltpu.VMEM),
        name="pack",
    )(keys, values, docs)
    far = shifted(packed, "ctx", 2)
    near = shifted(packed, "ctx", 1)
    place = lax.axis_index("ctx").astype(jnp.int32).reshape(1)
    sums = lambda dtype: jax.ShapeDtypeStruct((rows, 2 * width), dtype)
    dq, own_sums, near_sums, far_sums = pl.pallas_call(
        grads_kernel,
        out_shape=(jax.ShapeDtypeStruct(queries.shape, BF16), sums(F32), sums(BF16), sums(BF16)),
        in_specs=[pl.BlockSpec(memory_space=pltpu.SMEM)] + vmem(8),
        out_specs=tuple(vmem(4)),
        scratch_shapes=[pltpu.VMEM((HOPS + 1, rows, rows), F32)],
        compiler_params=pltpu.CompilerParams(vmem_limit_bytes=32 * 1024 * 1024),
        name="grads",
    )(place, queries, attn_out, arrived, log_sums, docs, packed, near, far)
    near_back = shifted(near_sums, "ctx", -1)
    far_back = shifted(far_sums, "ctx", -2)
    grad_keys, grad_values = pl.pallas_call(
        add_kernel,
        out_shape=(jax.ShapeDtypeStruct(keys.shape, BF16), jax.ShapeDtypeStruct(values.shape, BF16)),
        in_specs=vmem(3),
        out_specs=tuple(vmem(2)),
        name="add",
    )(own_sums, near_back, far_back)
    return dq, grad_keys, grad_values


def solution(mesh):
    placed = (
        P("section", "ctx", None),
        P("section", "ctx", None),
        P("section", "ctx", None),
        P("section", "ctx", None),
        P("section", None, "ctx"),
        P("section", "ctx", None),
        P("ctx"),
    )
    return jax.shard_map(
        per_device,
        mesh=mesh,
        in_specs=placed,
        out_specs=(P("section", "ctx", None), P("section", "ctx", None), P("section", "ctx", None)),
        check_vma=False,
    )
```

```python
import jax
import jax.numpy as jnp
from jax import lax
from jax.experimental import pallas as pl
from jax.experimental.pallas import tpu as pltpu
from jax.sharding import PartitionSpec as P

HOPS = 2
DOC_ROWS = 16
LOG2_E = 1.4426950408889634
MASKED = -1e30

F32 = jnp.float32
BF16 = jnp.bfloat16


def from_behind(block, axis, distance):
    devices = range(lax.axis_size(axis))
    route = [((i - distance) % len(devices), i) for i in devices]
    return lax.ppermute(block, axis, route)


def shifted(array, axis, by):
    devices = lax.axis_size(axis)
    pairs = [(i, i + by) for i in range(devices) if 0 <= i + by < devices]
    return lax.ppermute(array, axis, pairs)


def dot_nt(a, b):
    return lax.dot_general(a, b, (((1,), (1,)), ((), ())), preferred_element_type=F32)


def dot_nn(a, b):
    return lax.dot_general(a, b, (((1,), (0,)), ((), ())), preferred_element_type=F32)


def vmem(count):
    return [pl.BlockSpec(memory_space=pltpu.VMEM)] * count


def pack_kernel(keys, values, docs, packed, docs_here, sems):
    rows, width = keys.shape[1:]
    copies = [
        pltpu.make_async_copy(docs, docs_here, sems.at[0]),
        pltpu.make_async_copy(keys.at[0], packed.at[0:rows, 0:width], sems.at[1]),
        pltpu.make_async_copy(values.at[0], packed.at[0:rows, width : 2 * width], sems.at[2]),
    ]
    for copy in copies:
        copy.start()
    copies[0].wait()
    docs_row = (docs_here[...] + 1).astype(F32).astype(BF16)
    packed[rows : rows + DOC_ROWS, :] = jnp.broadcast_to(docs_row, (DOC_ROWS, docs_row.shape[1]))
    for copy in copies[1:]:
        copy.wait()


def column_of(row, width):
    rows = row.shape[1]
    column = jnp.transpose(jnp.broadcast_to(row, (width, rows)))
    return jnp.concatenate([column] * (rows // width), axis=1)


def block_grads(queries, grads, log_sums, delta_of, block, bias, score_grads, sums):
    rows = queries.shape[1]
    heads = log_sums.shape[1]
    width = queries.shape[2] // heads
    scale = float(width) ** -0.5
    sum_k = sum_v = None
    for head in range(heads):
        part = slice(head * width, (head + 1) * width)
        g = grads[0, :, part]
        delta = delta_of(head, part, g)
        q = queries[0, :, part]
        lse = log_sums[0, head : head + 1, :] * LOG2_E
        scores = dot_nt(block[0:rows, 0:width], q)
        weights = jnp.exp2(scores * (scale * LOG2_E) - lse + bias[...])
        weight_grads = dot_nt(block[0:rows, width : 2 * width], g)
        low = (weights * (weight_grads - delta)).astype(BF16)
        score_grads[head] = low
        term_v = dot_nn(weights.astype(BF16), g)
        term_k = dot_nn(low, q)
        sum_v = term_v if head == 0 else sum_v + term_v
        sum_k = term_k if head == 0 else sum_k + term_k
    sums[:, 0:width] = (sum_k * scale).astype(sums.dtype)
    sums[:, width : 2 * width] = sum_v.astype(sums.dtype)


def own_kernel(queries, attn_out, grads, log_sums, block, score_grads, sums, deltas, bias):
    rows = queries.shape[1]
    width = block.shape[1] // 2
    docs = block[rows : rows + DOC_ROWS, :].astype(F32)[0:1]
    key_at = lax.broadcasted_iota(jnp.int32, (rows, rows), 0)
    query_at = lax.broadcasted_iota(jnp.int32, (rows, rows), 1)
    bias[...] = jnp.where((column_of(docs, width) == docs) & (key_at <= query_at), 0.0, MASKED)
    one = jnp.ones((8, width), BF16)

    def delta_of(head, part, g):
        product = g.astype(F32) * attn_out[0, :, part].astype(F32)
        high = product.astype(BF16)
        low = (product - high.astype(F32)).astype(BF16)
        delta = (dot_nt(one, high) + dot_nt(one, low))[0:1]
        deltas[head : head + 1, :] = delta
        return delta

    block_grads(queries, grads, log_sums, delta_of, block, bias, score_grads, sums)


def hop_kernel(queries, grads, log_sums, deltas, own, block, before, score_grads, sums, bias):
    rows = queries.shape[1]
    width = block.shape[1] // 2
    docs = own[rows : rows + DOC_ROWS, :].astype(F32)[0:1]
    far_docs = block[rows : rows + DOC_ROWS, :].astype(F32)[0:1]
    bias[...] = jnp.where(column_of(far_docs, width) == docs, 0.0, MASKED)
    delta_of = lambda head, part, g: deltas[head : head + 1, :]
    block_grads(queries, grads, log_sums, delta_of, block, bias, score_grads, sums)


def query_kernel(own, near, far, own_grads, near_grads, far_grads, grad_queries):
    heads, rows = own_grads.shape[0:2]
    width = own.shape[1] // 2
    scale = float(width) ** -0.5
    turned = [jnp.transpose(block[0:rows, 0:width].astype(F32)).astype(BF16) for block in (own, near, far)]
    for head in range(heads):
        total = dot_nn(turned[0], own_grads[head]) + dot_nn(turned[1], near_grads[head]) + dot_nn(turned[2], far_grads[head])
        grad_queries[0, :, head * width : (head + 1) * width] = jnp.transpose(total * scale).astype(BF16)


def add_kernel(own_sums, near_sums, far_sums, grad_keys, grad_values):
    width = grad_keys.shape[2]
    total = own_sums[...] + near_sums[...].astype(F32) + far_sums[...].astype(F32)
    grad_keys[0] = total[:, 0:width].astype(BF16)
    grad_values[0] = total[:, width : 2 * width].astype(BF16)


def call(kernel, name, outs, args, flops=0, scratch=(), from_hbm=0, limit=8):
    args = [pltpu.with_memory_space_constraint(a, pltpu.HBM) for a in args[:from_hbm]] + list(args[from_hbm:])
    moved = sum(a.size * a.dtype.itemsize for a in args)
    return pl.pallas_call(
        kernel,
        out_shape=outs,
        in_specs=[pl.BlockSpec(memory_space=pltpu.HBM)] * from_hbm + vmem(len(args) - from_hbm),
        out_specs=tuple(vmem(len(outs))),
        scratch_shapes=list(scratch),
        compiler_params=pltpu.CompilerParams(vmem_limit_bytes=limit * 1024 * 1024),
        cost_estimate=pl.CostEstimate(flops=flops, bytes_accessed=moved, transcendentals=0),
        name=name,
    )(*args)


def per_device(queries, keys, values, attn_out, log_sums, grad_held, doc_ids):
    rows, width = keys.shape[1:]
    heads = log_sums.shape[1]
    shape = jax.ShapeDtypeStruct
    flops = 2 * heads * rows * rows * width
    bias = pltpu.VMEM((rows, rows), F32)
    score_grads = shape((heads, rows, rows), BF16)
    sums = lambda dtype: shape((rows, 2 * width), dtype)

    grads = from_behind(grad_held, "section", -1)
    (own,) = call(
        pack_kernel,
        "pack",
        (shape((rows + DOC_ROWS, 2 * width), BF16),),
        (keys, values, doc_ids.reshape(1, rows)),
        40 * flops,
        [pltpu.VMEM((1, rows), jnp.int32), pltpu.SemaphoreType.DMA((3,))],
        3,
    )
    near = shifted(own, "ctx", 1)
    far = shifted(own, "ctx", 2)
    own_grads, own_sums, deltas = call(
        own_kernel, "own_block", (score_grads, sums(F32), shape((heads, rows), F32)), (queries, attn_out, grads, log_sums, own), 4 * flops, [bias]
    )
    hop = lambda name, block, before: call(hop_kernel, name, (score_grads, sums(BF16)), (queries, grads, log_sums, deltas, own, block, before), 4 * flops, [bias])
    near_grads, near_sums = hop("near_block", near, own_sums)
    near_back = shifted(near_sums, "ctx", -1)
    far_grads, far_sums = hop("far_block", far, near_sums)
    far_back = shifted(far_sums, "ctx", -2)
    (grad_queries,) = call(query_kernel, "query_grads", (shape(queries.shape, BF16),), (own, near, far, own_grads, near_grads, far_grads), 3 * flops)
    grad_keys, grad_values = call(add_kernel, "add", (shape(keys.shape, BF16), shape(values.shape, BF16)), (own_sums, near_back, far_back))
    return grad_queries, grad_keys, grad_values


def solution(mesh):
    placed = (
        P("section", "ctx", None),
        P("section", "ctx", None),
        P("section", "ctx", None),
        P("section", "ctx", None),
        P("section", None, "ctx"),
        P("section", "ctx", None),
        P("ctx"),
    )
    return jax.shard_map(
        per_device,
        mesh=mesh,
        in_specs=placed,
        out_specs=(P("section", "ctx", None), P("section", "ctx", None), P("section", "ctx", None)),
        check_vma=False,
    )
```

```python
import jax
import jax.numpy as jnp
from jax import lax
from jax.experimental import pallas as pl
from jax.experimental.pallas import tpu as pltpu
from jax.sharding import PartitionSpec as P

HOPS = 2
DOC_ROWS = 16
LOG2_E = 1.4426950408889634
MASKED = -1e30

F32 = jnp.float32
BF16 = jnp.bfloat16


def from_behind(block, axis, distance):
    devices = range(lax.axis_size(axis))
    route = [((i - distance) % len(devices), i) for i in devices]
    return lax.ppermute(block, axis, route)


def shifted(array, axis, by):
    devices = lax.axis_size(axis)
    pairs = [(i, i + by) for i in range(devices) if 0 <= i + by < devices]
    return lax.ppermute(array, axis, pairs)


def dot_nt(a, b):
    return lax.dot_general(a, b, (((1,), (1,)), ((), ())), preferred_element_type=F32)


def dot_nn(a, b):
    return lax.dot_general(a, b, (((1,), (0,)), ((), ())), preferred_element_type=F32)


def vmem(count):
    return [pl.BlockSpec(memory_space=pltpu.VMEM)] * count


def pack_kernel(keys, values, docs, packed, docs_here, sems):
    rows, width = keys.shape[1:]
    copies = [
        pltpu.make_async_copy(docs, docs_here, sems.at[0]),
        pltpu.make_async_copy(keys.at[0], packed.at[0:rows, 0:width], sems.at[1]),
        pltpu.make_async_copy(values.at[0], packed.at[0:rows, width : 2 * width], sems.at[2]),
    ]
    for copy in copies:
        copy.start()
    copies[0].wait()
    docs_row = (docs_here[...] + 1).astype(F32).astype(BF16)
    packed[rows : rows + DOC_ROWS, :] = jnp.broadcast_to(docs_row, (DOC_ROWS, docs_row.shape[1]))
    for copy in copies[1:]:
        copy.wait()


def column_of(row, width):
    rows = row.shape[1]
    column = jnp.transpose(jnp.broadcast_to(row, (width, rows)))
    return jnp.concatenate([column] * (rows // width), axis=1)


def block_grads(queries, grads, log_sums, delta_of, block, bias, score_grads, weights_low, sums):
    rows = queries.shape[1]
    heads = log_sums.shape[1]
    width = queries.shape[2] // heads
    scale = float(width) ** -0.5
    parts = [slice(head * width, (head + 1) * width) for head in range(heads)]
    for head, part in enumerate(parts):
        columns = slice(head * rows, (head + 1) * rows)
        g = grads[0, :, part]
        delta = delta_of(head, part, g)
        lse = log_sums[0, head : head + 1, :] * LOG2_E
        scores = dot_nt(block[0:rows, 0:width], queries[0, :, part])
        weights = jnp.exp2(scores * (scale * LOG2_E) - lse + bias[...])
        weight_grads = dot_nt(block[0:rows, width : 2 * width], g)
        score_grads[:, columns] = (weights * (weight_grads - delta)).astype(BF16)
        weights_low[:, columns] = weights.astype(BF16)
    stacked = lambda ref: jnp.concatenate([ref[0, :, part] for part in parts], axis=0)
    sums[:, 0:width] = (dot_nn(score_grads[...], stacked(queries)) * scale).astype(sums.dtype)
    sums[:, width : 2 * width] = dot_nn(weights_low[...], stacked(grads)).astype(sums.dtype)


def own_kernel(queries, attn_out, grads, log_sums, block, score_grads, sums, deltas, block_again, bias, weights_low):
    rows = queries.shape[1]
    width = block.shape[1] // 2
    block_again[...] = block[...]
    docs = block[rows : rows + DOC_ROWS, :].astype(F32)[0:1]
    key_at = lax.broadcasted_iota(jnp.int32, (rows, rows), 0)
    query_at = lax.broadcasted_iota(jnp.int32, (rows, rows), 1)
    bias[...] = jnp.where((column_of(docs, width) == docs) & (key_at <= query_at), 0.0, MASKED)
    one = jnp.ones((8, width), BF16)

    def delta_of(head, part, g):
        product = g.astype(F32) * attn_out[0, :, part].astype(F32)
        high = product.astype(BF16)
        low = (product - high.astype(F32)).astype(BF16)
        delta = (dot_nt(one, high) + dot_nt(one, low))[0:1]
        deltas[head : head + 1, :] = delta
        return delta

    block_grads(queries, grads, log_sums, delta_of, block, bias, score_grads, weights_low, sums)


def hop_kernel(queries, grads, log_sums, deltas, own, block, before, score_grads, sums, bias, weights_low):
    rows = queries.shape[1]
    width = block.shape[1] // 2
    docs = own[rows : rows + DOC_ROWS, :].astype(F32)[0:1]
    far_docs = block[rows : rows + DOC_ROWS, :].astype(F32)[0:1]
    bias[...] = jnp.where(column_of(far_docs, width) == docs, 0.0, MASKED)
    delta_of = lambda head, part, g: deltas[head : head + 1, :]
    block_grads(queries, grads, log_sums, delta_of, block, bias, score_grads, weights_low, sums)


def query_kernel(own, near, far, own_grads, near_grads, far_grads, grad_queries):
    rows = own_grads.shape[0]
    heads = own_grads.shape[1] // rows
    width = own.shape[1] // 2
    scale = float(width) ** -0.5
    turned = [jnp.transpose(block[0:rows, 0:width].astype(F32)).astype(BF16) for block in (own, near, far)]
    for head in range(heads):
        columns = slice(head * rows, (head + 1) * rows)
        total = dot_nn(turned[0], own_grads[:, columns]) + dot_nn(turned[1], near_grads[:, columns]) + dot_nn(turned[2], far_grads[:, columns])
        grad_queries[0, :, head * width : (head + 1) * width] = jnp.transpose(total * scale).astype(BF16)


def add_kernel(own_sums, near_sums, far_sums, grad_keys, grad_values):
    width = grad_keys.shape[2]
    total = own_sums[...] + near_sums[...].astype(F32) + far_sums[...].astype(F32)
    grad_keys[0] = total[:, 0:width].astype(BF16)
    grad_values[0] = total[:, width : 2 * width].astype(BF16)


def call(kernel, name, outs, args, flops=0, scratch=(), from_hbm=0, limit=8):
    args = [pltpu.with_memory_space_constraint(a, pltpu.HBM) for a in args[:from_hbm]] + list(args[from_hbm:])
    moved = sum(a.size * a.dtype.itemsize for a in args)
    return pl.pallas_call(
        kernel,
        out_shape=outs,
        in_specs=[pl.BlockSpec(memory_space=pltpu.HBM)] * from_hbm + vmem(len(args) - from_hbm),
        out_specs=tuple(vmem(len(outs))),
        scratch_shapes=list(scratch),
        compiler_params=pltpu.CompilerParams(vmem_limit_bytes=limit * 1024 * 1024),
        cost_estimate=pl.CostEstimate(flops=flops, bytes_accessed=moved, transcendentals=0),
        name=name,
    )(*args)


def per_device(queries, keys, values, attn_out, log_sums, grad_held, doc_ids):
    rows, width = keys.shape[1:]
    heads = log_sums.shape[1]
    shape = jax.ShapeDtypeStruct
    flops = 2 * heads * rows * rows * width
    score_grads = shape((rows, heads * rows), BF16)
    scratch = [pltpu.VMEM((rows, rows), F32), pltpu.VMEM((rows, heads * rows), BF16)]
    sums = lambda dtype: shape((rows, 2 * width), dtype)

    grads = from_behind(grad_held, "section", -1)
    (own,) = call(
        pack_kernel,
        "pack",
        (shape((rows + DOC_ROWS, 2 * width), BF16),),
        (keys, values, doc_ids.reshape(1, rows)),
        40 * flops,
        [pltpu.VMEM((1, rows), jnp.int32), pltpu.SemaphoreType.DMA((3,))],
        3,
    )
    near = shifted(own, "ctx", 1)
    own_grads, own_sums, deltas, own_again = call(
        own_kernel,
        "own_block",
        (score_grads, sums(F32), shape((heads, rows), F32), shape(own.shape, BF16)),
        (queries, attn_out, grads, log_sums, own),
        4 * flops,
        scratch,
    )
    far = shifted(own_again, "ctx", 2)
    hop = lambda name, block, before: call(hop_kernel, name, (score_grads, sums(BF16)), (queries, grads, log_sums, deltas, own, block, before), 4 * flops, scratch)
    near_grads, near_sums = hop("near_block", near, own_sums)
    near_back = shifted(near_sums, "ctx", -1)
    far_grads, far_sums = hop("far_block", far, near_sums)
    far_back = shifted(far_sums, "ctx", -2)
    (grad_queries,) = call(query_kernel, "query_grads", (shape(queries.shape, BF16),), (own, near, far, own_grads, near_grads, far_grads), 3 * flops)
    grad_keys, grad_values = call(add_kernel, "add", (shape(keys.shape, BF16), shape(values.shape, BF16)), (own_sums, near_back, far_back))
    return grad_queries, grad_keys, grad_values


def solution(mesh):
    placed = (
        P("section", "ctx", None),
        P("section", "ctx", None),
        P("section", "ctx", None),
        P("section", "ctx", None),
        P("section", None, "ctx"),
        P("section", "ctx", None),
        P("ctx"),
    )
    return jax.shard_map(
        per_device,
        mesh=mesh,
        in_specs=placed,
        out_specs=(P("section", "ctx", None), P("section", "ctx", None), P("section", "ctx", None)),
        check_vma=False,
    )
```

```python
import functools

import jax
import jax.numpy as jnp
from jax import lax
from jax.experimental import pallas as pl
from jax.experimental.pallas import tpu as pltpu
from jax.sharding import PartitionSpec as P

HOPS = 2
DOC_ROWS = 16
BACK_STRIDE = 4
LOG2_E = 1.4426950408889634
MASKED = -1e30

F32 = jnp.float32
BF16 = jnp.bfloat16


def from_behind(block, axis, distance):
    devices = range(lax.axis_size(axis))
    route = [((i - distance) % len(devices), i) for i in devices]
    return lax.ppermute(block, axis, route)


def shifted(array, axis, by):
    devices = lax.axis_size(axis)
    pairs = [(i, i + by) for i in range(devices) if 0 <= i + by < devices]
    return lax.ppermute(array, axis, pairs)


def full_routes(sections, shards, by, parity):
    route = {}
    for at in range(0, sections, 2):
        there, back = at + parity, at + 1 - parity
        for c in range(shards - by):
            route[there, c] = (there, c + by)
        free = set(range(shards))
        for last in range(shards - by, shards):
            first = last - shards + by
            way = [(there, last)] + [(back, c) for c in range(last, by - 1, -BACK_STRIDE)] + [(back, first), (there, first)]
            free -= {c for section, c in way if section == back}
            route.update(zip(way, way[1:]))
        for lane in range(BACK_STRIDE):
            rest = [c for c in sorted(free) if c % BACK_STRIDE == lane]
            pairs = [(c, c + 1) for c in rest if c + 1 in free] if by > 1 else []
            if by == 1:
                pairs = list(zip(rest[0::2], rest[1::2])) if len(rest) % 2 == 0 else []
                if not pairs:
                    route.update({(back, c): (back, rest[k - len(rest) + 1]) for k, c in enumerate(rest)})
            for c, d in pairs:
                route.update({(back, c): (back, d), (back, d): (back, c)})
    full = sections * shards
    whole = len(route) == full and len(set(route.values())) == full and all(a != b for a, b in route.items())
    return [(a * shards + c, b * shards + d) for (a, c), (b, d) in sorted(route.items())] if whole else None


def behind(block, by):
    sections, shards = lax.axis_size("section"), lax.axis_size("ctx")
    routes = [full_routes(sections, shards, by, parity) for parity in (0, 1)] if sections % 2 == 0 and shards >= 4 * BACK_STRIDE else [None]
    if None in routes:
        return [shifted(block, "ctx", by)]
    return [lax.ppermute(block, ("section", "ctx"), route) for route in routes]


def dot_nt(a, b):
    return lax.dot_general(a, b, (((1,), (1,)), ((), ())), preferred_element_type=F32)


def dot_nn(a, b):
    return lax.dot_general(a, b, (((1,), (0,)), ((), ())), preferred_element_type=F32)


def vmem(count):
    return [pl.BlockSpec(memory_space=pltpu.VMEM)] * count


def pack_kernel(keys, values, docs, packed, docs_here, sems):
    rows, width = keys.shape[1:]
    copies = [
        pltpu.make_async_copy(docs, docs_here, sems.at[0]),
        pltpu.make_async_copy(keys.at[0], packed.at[0:rows, 0:width], sems.at[1]),
        pltpu.make_async_copy(values.at[0], packed.at[0:rows, width : 2 * width], sems.at[2]),
    ]
    for copy in copies:
        copy.start()
    copies[0].wait()
    docs_row = (docs_here[...] + 1).astype(F32).astype(BF16)
    packed[rows : rows + DOC_ROWS, :] = jnp.broadcast_to(docs_row, (DOC_ROWS, docs_row.shape[1]))
    for copy in copies[1:]:
        copy.wait()


def column_of(row, width):
    rows = row.shape[1]
    column = jnp.transpose(jnp.broadcast_to(row, (width, rows)))
    return jnp.concatenate([column] * (rows // width), axis=1)


def block_grads(queries, grads, log_sums, delta_of, block, bias, score_grads, weights_low, sums):
    rows = queries.shape[1]
    heads = log_sums.shape[1]
    width = queries.shape[2] // heads
    scale = float(width) ** -0.5
    parts = [slice(head * width, (head + 1) * width) for head in range(heads)]
    for head, part in enumerate(parts):
        columns = slice(head * rows, (head + 1) * rows)
        g = grads[0, :, part]
        delta = delta_of(head, part, g)
        lse = log_sums[0, head : head + 1, :] * LOG2_E
        scores = dot_nt(block[0:rows, 0:width], queries[0, :, part])
        weights = jnp.exp2(scores * (scale * LOG2_E) - lse + bias[...])
        weight_grads = dot_nt(block[0:rows, width : 2 * width], g)
        score_grads[:, columns] = (weights * (weight_grads - delta)).astype(BF16)
        weights_low[:, columns] = weights.astype(BF16)
    stacked = lambda ref: jnp.concatenate([ref[0, :, part] for part in parts], axis=0)
    sums[:, 0:width] = (dot_nn(score_grads[...], stacked(queries)) * scale).astype(sums.dtype)
    sums[:, width : 2 * width] = dot_nn(weights_low[...], stacked(grads)).astype(sums.dtype)


def own_kernel(queries, attn_out, grads, log_sums, block, score_grads, sums, deltas, block_again, bias, weights_low):
    rows = queries.shape[1]
    width = block.shape[1] // 2
    block_again[...] = block[...]
    docs = block[rows : rows + DOC_ROWS, :].astype(F32)[0:1]
    key_at = lax.broadcasted_iota(jnp.int32, (rows, rows), 0)
    query_at = lax.broadcasted_iota(jnp.int32, (rows, rows), 1)
    bias[...] = jnp.where((column_of(docs, width) == docs) & (key_at <= query_at), 0.0, MASKED)
    one = jnp.ones((8, width), BF16)

    def delta_of(head, part, g):
        product = g.astype(F32) * attn_out[0, :, part].astype(F32)
        high = product.astype(BF16)
        low = (product - high.astype(F32)).astype(BF16)
        delta = (dot_nt(one, high) + dot_nt(one, low))[0:1]
        deltas[head : head + 1, :] = delta
        return delta

    block_grads(queries, grads, log_sums, delta_of, block, bias, score_grads, weights_low, sums)


def hop_kernel(hop, queries, grads, log_sums, deltas, own, before, *refs):
    candidates, (score_grads, sums, block, bias, weights_low) = refs[:-5], refs[-5:]
    rows = queries.shape[1]
    width = own.shape[1] // 2
    if len(candidates) == 1:
        block[...] = candidates[0][...]
    for parity, candidate in enumerate(candidates[: len(candidates) // 2 * 2]):

        @pl.when(lax.axis_index("section") % 2 == parity)
        def _():
            block[...] = candidate[...]

    docs = own[rows : rows + DOC_ROWS, :].astype(F32)[0:1]
    far_docs = block[rows : rows + DOC_ROWS, :].astype(F32)[0:1]
    far_docs = jnp.where(lax.axis_index("ctx") >= hop, far_docs, 0.0)
    bias[...] = jnp.where(column_of(far_docs, width) == docs, 0.0, MASKED)
    delta_of = lambda head, part, g: deltas[head : head + 1, :]
    block_grads(queries, grads, log_sums, delta_of, block, bias, score_grads, weights_low, sums)


def query_kernel(own, near, far, own_grads, near_grads, far_grads, grad_queries):
    rows = own_grads.shape[0]
    heads = own_grads.shape[1] // rows
    width = own.shape[1] // 2
    scale = float(width) ** -0.5
    turned = [jnp.transpose(block[0:rows, 0:width].astype(F32)).astype(BF16) for block in (own, near, far)]
    for head in range(heads):
        columns = slice(head * rows, (head + 1) * rows)
        total = dot_nn(turned[0], own_grads[:, columns]) + dot_nn(turned[1], near_grads[:, columns]) + dot_nn(turned[2], far_grads[:, columns])
        grad_queries[0, :, head * width : (head + 1) * width] = jnp.transpose(total * scale).astype(BF16)


def add_kernel(own_sums, near_sums, far_sums, grad_keys, grad_values):
    width = grad_keys.shape[2]
    total = own_sums[...] + near_sums[...].astype(F32) + far_sums[...].astype(F32)
    grad_keys[0] = total[:, 0:width].astype(BF16)
    grad_values[0] = total[:, width : 2 * width].astype(BF16)


def call(kernel, name, outs, args, flops=0, scratch=(), from_hbm=0, limit=8):
    args = [pltpu.with_memory_space_constraint(a, pltpu.HBM) for a in args[:from_hbm]] + list(args[from_hbm:])
    moved = sum(a.size * a.dtype.itemsize for a in args)
    return pl.pallas_call(
        kernel,
        out_shape=outs,
        in_specs=[pl.BlockSpec(memory_space=pltpu.HBM)] * from_hbm + vmem(len(args) - from_hbm),
        out_specs=tuple(vmem(len(outs))),
        scratch_shapes=list(scratch),
        compiler_params=pltpu.CompilerParams(vmem_limit_bytes=limit * 1024 * 1024),
        cost_estimate=pl.CostEstimate(flops=flops, bytes_accessed=moved, transcendentals=0),
        name=name,
    )(*args)


def per_device(queries, keys, values, attn_out, log_sums, grad_held, doc_ids):
    rows, width = keys.shape[1:]
    heads = log_sums.shape[1]
    shape = jax.ShapeDtypeStruct
    flops = 2 * heads * rows * rows * width
    score_grads = shape((rows, heads * rows), BF16)
    scratch = [pltpu.VMEM((rows, rows), F32), pltpu.VMEM((rows, heads * rows), BF16)]
    sums = lambda dtype: shape((rows, 2 * width), dtype)

    grads = from_behind(grad_held, "section", -1)
    (own,) = call(
        pack_kernel,
        "pack",
        (shape((rows + DOC_ROWS, 2 * width), BF16),),
        (keys, values, doc_ids.reshape(1, rows)),
        40 * flops,
        [pltpu.VMEM((1, rows), jnp.int32), pltpu.SemaphoreType.DMA((3,))],
        3,
    )
    near = behind(own, 1)
    own_grads, own_sums, deltas, own_again = call(
        own_kernel,
        "own_block",
        (score_grads, sums(F32), shape((heads, rows), F32), shape(own.shape, BF16)),
        (queries, attn_out, grads, log_sums, own),
        4 * flops,
        scratch,
    )
    far = behind(own_again, 2)
    def block_of(name, hop, before, candidates):
        outs = (score_grads, sums(BF16), shape(own.shape, BF16))
        return call(
            functools.partial(hop_kernel, hop), name, outs, (queries, grads, log_sums, deltas, own, before, *candidates), 4 * flops, scratch
        )

    near_grads, near_sums, near = block_of("near_block", 1, own_sums, near)
    near_back = shifted(near_sums, "ctx", -1)
    far_grads, far_sums, far = block_of("far_block", 2, near_sums, far)
    far_back = shifted(far_sums, "ctx", -2)
    (grad_queries,) = call(query_kernel, "query_grads", (shape(queries.shape, BF16),), (own, near, far, own_grads, near_grads, far_grads), 3 * flops)
    grad_keys, grad_values = call(add_kernel, "add", (shape(keys.shape, BF16), shape(values.shape, BF16)), (own_sums, near_back, far_back))
    return grad_queries, grad_keys, grad_values


def solution(mesh):
    placed = (
        P("section", "ctx", None),
        P("section", "ctx", None),
        P("section", "ctx", None),
        P("section", "ctx", None),
        P("section", None, "ctx"),
        P("section", "ctx", None),
        P("ctx"),
    )
    return jax.shard_map(
        per_device,
        mesh=mesh,
        in_specs=placed,
        out_specs=(P("section", "ctx", None), P("section", "ctx", None), P("section", "ctx", None)),
        check_vma=False,
    )
```

```python
import functools

import jax
import jax.numpy as jnp
from jax import lax
from jax.experimental import pallas as pl
from jax.experimental.pallas import tpu as pltpu
from jax.sharding import PartitionSpec as P

HOPS = 2
DOC_ROWS = 16
LAST_ROW = 8
COUNT_ROW = 9
FACT_ROWS = 8
NONE, FEW_KEYS, FEW_QUERIES, ALL = range(4)
BACK_STRIDE = 4
LOG2_E = 1.4426950408889634
MASKED = -1e30

F32 = jnp.float32
BF16 = jnp.bfloat16


def from_behind(block, axis, distance):
    devices = range(lax.axis_size(axis))
    route = [((i - distance) % len(devices), i) for i in devices]
    return lax.ppermute(block, axis, route)


def shifted(array, axis, by):
    devices = lax.axis_size(axis)
    pairs = [(i, i + by) for i in range(devices) if 0 <= i + by < devices]
    return lax.ppermute(array, axis, pairs)


def full_routes(sections, shards, by, parity):
    route = {}
    for at in range(0, sections, 2):
        there, back = at + parity, at + 1 - parity
        for c in range(shards - by):
            route[there, c] = (there, c + by)
        free = set(range(shards))
        for last in range(shards - by, shards):
            first = last - shards + by
            way = [(there, last)] + [(back, c) for c in range(last, by - 1, -BACK_STRIDE)] + [(back, first), (there, first)]
            free -= {c for section, c in way if section == back}
            route.update(zip(way, way[1:]))
        for lane in range(BACK_STRIDE):
            rest = [c for c in sorted(free) if c % BACK_STRIDE == lane]
            pairs = [(c, c + 1) for c in rest if c + 1 in free] if by > 1 else []
            if by == 1:
                pairs = list(zip(rest[0::2], rest[1::2])) if len(rest) % 2 == 0 else []
                if not pairs:
                    route.update({(back, c): (back, rest[k - len(rest) + 1]) for k, c in enumerate(rest)})
            for c, d in pairs:
                route.update({(back, c): (back, d), (back, d): (back, c)})
    full = sections * shards
    whole = len(route) == full and len(set(route.values())) == full and all(a != b for a, b in route.items())
    return [(a * shards + c, b * shards + d) for (a, c), (b, d) in sorted(route.items())] if whole else None


def behind(block, by):
    sections, shards = lax.axis_size("section"), lax.axis_size("ctx")
    routes = [full_routes(sections, shards, by, parity) for parity in (0, 1)] if sections % 2 == 0 and shards >= 4 * BACK_STRIDE else [None]
    if None in routes:
        return [shifted(block, "ctx", by)]
    return [lax.ppermute(block, ("section", "ctx"), route) for route in routes]


def dot_nt(a, b):
    return lax.dot_general(a, b, (((1,), (1,)), ((), ())), preferred_element_type=F32)


def dot_nn(a, b):
    return lax.dot_general(a, b, (((1,), (0,)), ((), ())), preferred_element_type=F32)


def pack_kernel(keys, values, docs, packed, docs_here, sems):
    rows, width = keys.shape[1:]
    copies = [
        pltpu.make_async_copy(docs, docs_here, sems.at[0]),
        pltpu.make_async_copy(keys.at[0], packed.at[0:rows, 0:width], sems.at[1]),
        pltpu.make_async_copy(values.at[0], packed.at[0:rows, width : 2 * width], sems.at[2]),
    ]
    for copy in copies:
        copy.start()
    copies[0].wait()
    docs_row = docs_here[...]
    last = jnp.max(docs_row, axis=1, keepdims=True)
    last_count = jnp.sum((docs_row == last).astype(F32), axis=1, keepdims=True)
    row_at = lax.broadcasted_iota(jnp.int32, (DOC_ROWS, rows), 0)
    table = jnp.where(row_at == LAST_ROW, last.astype(F32) + 1, jnp.where(row_at == COUNT_ROW, last_count, docs_row.astype(F32) + 1))
    packed[rows : rows + DOC_ROWS, :] = table.astype(BF16)
    for copy in copies[1:]:
        copy.wait()


def column_of(row, width):
    rows = row.shape[1]
    column = jnp.transpose(jnp.broadcast_to(row, (width, rows)))
    return jnp.concatenate([column] * (rows // width), axis=1)


def block_grads(queries, grads, log_sums, delta_of, block, bias, score_grads, weights_low, sums, first_key, query_rows):
    rows = queries.shape[1]
    heads = log_sums.shape[1]
    width = queries.shape[2] // heads
    scale = float(width) ** -0.5
    beside = rows // query_rows
    key_rows = slice(first_key, rows)
    side = lambda pieces: pieces[0] if len(pieces) == 1 else jnp.concatenate(pieces, axis=1)
    under = lambda pieces: pieces[0] if len(pieces) == 1 else jnp.concatenate(pieces, axis=0)
    part = lambda ref, head: ref[0, 0:query_rows, head * width : (head + 1) * width]
    columns = lambda head: slice(head * rows, head * rows + query_rows)
    masked = side([bias[key_rows, 0:query_rows]] * beside)
    for head in range(0, heads, beside):
        group = range(head, head + beside)
        g = under([part(grads, h) for h in group])
        delta = side([delta_of(h, part(grads, h))[:, 0:query_rows] for h in group])
        lse = side([log_sums[0, h : h + 1, 0:query_rows] for h in group]) * LOG2_E
        scores = dot_nt(block[key_rows, 0:width], under([part(queries, h) for h in group]))
        weights = jnp.exp2(scores * (scale * LOG2_E) - lse + masked)
        weight_grads = dot_nt(block[key_rows, width : 2 * width], g)
        low = (weights * (weight_grads - delta)).astype(BF16)
        weights = weights.astype(BF16)
        for at, h in enumerate(group):
            here = slice(at * query_rows, (at + 1) * query_rows)
            score_grads[key_rows, columns(h)] = low[:, here]
            weights_low[key_rows, columns(h)] = weights[:, here]
    everything = lambda ref: ref[key_rows, :] if beside == 1 else side([ref[key_rows, columns(h)] for h in range(heads)])
    stacked = lambda ref: under([part(ref, h) for h in range(heads)])
    sums[key_rows, 0:width] = (dot_nn(everything(score_grads), stacked(queries)) * scale).astype(sums.dtype)
    sums[key_rows, width : 2 * width] = dot_nn(everything(weights_low), stacked(grads)).astype(sums.dtype)


def own_kernel(queries, attn_out, grads, log_sums, block, score_grads, sums, deltas, block_again, bias, weights_low):
    rows = queries.shape[1]
    width = block.shape[1] // 2
    block_again[...] = block[...]
    docs = block[rows : rows + DOC_ROWS, :].astype(F32)[0:1]
    key_at = lax.broadcasted_iota(jnp.int32, (rows, rows), 0)
    query_at = lax.broadcasted_iota(jnp.int32, (rows, rows), 1)
    bias[...] = jnp.where((column_of(docs, width) == docs) & (key_at <= query_at), 0.0, MASKED)
    first_count = jnp.sum((docs == docs[:, 0:1]).astype(F32), axis=1, keepdims=True)
    deltas[log_sums.shape[1] :, :] = jnp.broadcast_to(first_count, (FACT_ROWS, rows))
    one = jnp.ones((8, width), BF16)

    def delta_of(head, g):
        product = g.astype(F32) * attn_out[0, :, head * width : (head + 1) * width].astype(F32)
        high = product.astype(BF16)
        low = (product - high.astype(F32)).astype(BF16)
        delta = (dot_nt(one, high) + dot_nt(one, low))[0:1]
        deltas[head : head + 1, :] = delta
        return delta

    block_grads(queries, grads, log_sums, delta_of, block, bias, score_grads, weights_low, sums, 0, rows)


def hop_kernel(hop, queries, grads, log_sums, deltas, own, before, *refs):
    candidates, (score_grads, sums, block, bias, weights_low) = refs[:-5], refs[-5:]
    rows = queries.shape[1]
    half = rows // 2
    if len(candidates) == 1:
        block[...] = candidates[0][...]
    for parity, candidate in enumerate(candidates[: len(candidates) // 2 * 2]):

        @pl.when(lax.axis_index("section") % 2 == parity)
        def _():
            block[...] = candidate[...]

    docs = own[rows : rows + DOC_ROWS, :].astype(F32)[0:1]
    table = block[rows : rows + DOC_ROWS, :].astype(F32)
    same = (table[LAST_ROW : LAST_ROW + 1] == docs[:, 0:1]) & (lax.axis_index("ctx") >= hop)
    key_count = jnp.where(same, table[COUNT_ROW : COUNT_ROW + 1], 0.0)
    query_count = deltas[log_sums.shape[1] : log_sums.shape[1] + 1, :]
    key_at = lax.broadcasted_iota(jnp.int32, (rows, rows), 0).astype(F32)
    bias[...] = jnp.where((key_at >= rows - key_count) & (docs == docs[:, 0:1]), 0.0, MASKED)
    some = jnp.where(query_count <= half, FEW_QUERIES, ALL)
    mode = jnp.where(key_count == 0, NONE, jnp.where(key_count <= half, FEW_KEYS, some))[0, 0]
    delta_of = lambda head, g: deltas[head : head + 1, :]
    work = functools.partial(block_grads, queries, grads, log_sums, delta_of, block, bias, score_grads, weights_low, sums)

    @pl.when(mode == NONE)
    def _():
        score_grads[...] = jnp.zeros_like(score_grads)
        sums[...] = jnp.zeros_like(sums)

    @pl.when(mode == FEW_KEYS)
    def _():
        score_grads[0:half, :] = jnp.zeros((half, score_grads.shape[1]), BF16)
        sums[0:half, :] = jnp.zeros((half, sums.shape[1]), BF16)
        work(half, rows)

    @pl.when(mode == FEW_QUERIES)
    def _():
        for head in range(score_grads.shape[1] // rows):
            score_grads[:, head * rows + half : (head + 1) * rows] = jnp.zeros((rows, rows - half), BF16)
        work(0, half)

    if hop < HOPS:

        @pl.when(mode == ALL)
        def _():
            work(0, rows)


def query_kernel(own, near, far, own_grads, near_grads, far_grads, grad_queries):
    rows = own_grads.shape[0]
    heads = own_grads.shape[1] // rows
    width = own.shape[1] // 2
    scale = float(width) ** -0.5
    turned = [jnp.transpose(block[0:rows, 0:width].astype(F32)).astype(BF16) for block in (own, near, far)]
    for head in range(heads):
        columns = slice(head * rows, (head + 1) * rows)
        total = dot_nn(turned[0], own_grads[:, columns]) + dot_nn(turned[1], near_grads[:, columns]) + dot_nn(turned[2], far_grads[:, columns])
        grad_queries[0, :, head * width : (head + 1) * width] = jnp.transpose(total * scale).astype(BF16)


def add_kernel(own_sums, near_sums, far_sums, grad_keys, grad_values):
    width = grad_keys.shape[2]
    total = own_sums[...] + near_sums[...].astype(F32) + far_sums[...].astype(F32)
    grad_keys[0] = total[:, 0:width].astype(BF16)
    grad_values[0] = total[:, width : 2 * width].astype(BF16)


def call(kernel, name, outs, args, flops=0, scratch=(), from_hbm=0, limit=8):
    args = [pltpu.with_memory_space_constraint(a, pltpu.HBM) for a in args[:from_hbm]] + list(args[from_hbm:])
    moved = sum(a.size * a.dtype.itemsize for a in args)
    vmem = lambda count: [pl.BlockSpec(memory_space=pltpu.VMEM)] * count
    return pl.pallas_call(
        kernel,
        out_shape=outs,
        in_specs=[pl.BlockSpec(memory_space=pltpu.HBM)] * from_hbm + vmem(len(args) - from_hbm),
        out_specs=tuple(vmem(len(outs))),
        scratch_shapes=list(scratch),
        compiler_params=pltpu.CompilerParams(vmem_limit_bytes=limit * 1024 * 1024),
        cost_estimate=pl.CostEstimate(flops=flops, bytes_accessed=moved, transcendentals=0),
        name=name,
    )(*args)


def per_device(queries, keys, values, attn_out, log_sums, grad_held, doc_ids):
    rows, width = keys.shape[1:]
    heads = log_sums.shape[1]
    shape = jax.ShapeDtypeStruct
    flops = 2 * heads * rows * rows * width
    score_grads = shape((rows, heads * rows), BF16)
    scratch = [pltpu.VMEM((rows, rows), F32), pltpu.VMEM((rows, heads * rows), BF16)]
    sums = lambda dtype: shape((rows, 2 * width), dtype)

    grads = from_behind(grad_held, "section", -1)
    (own,) = call(
        pack_kernel,
        "pack",
        (shape((rows + DOC_ROWS, 2 * width), BF16),),
        (keys, values, doc_ids.reshape(1, rows)),
        40 * flops,
        [pltpu.VMEM((1, rows), jnp.int32), pltpu.SemaphoreType.DMA((3,))],
        3,
    )
    near = behind(own, 1)
    own_grads, own_sums, deltas, own_again = call(
        own_kernel,
        "own_block",
        (score_grads, sums(F32), shape((heads + FACT_ROWS, rows), F32), shape(own.shape, BF16)),
        (queries, attn_out, grads, log_sums, own),
        4 * flops,
        scratch,
    )
    far = behind(own_again, 2)
    def block_of(name, hop, before, candidates):
        outs = (score_grads, sums(BF16), shape(own.shape, BF16))
        return call(
            functools.partial(hop_kernel, hop), name, outs, (queries, grads, log_sums, deltas, own, before, *candidates), 4 * flops, scratch
        )

    near_grads, near_sums, near = block_of("near_block", 1, own_sums, near)
    near_back = shifted(near_sums, "ctx", -1)
    far_grads, far_sums, far = block_of("far_block", 2, near_sums, far)
    far_back = shifted(far_sums, "ctx", -2)
    (grad_queries,) = call(query_kernel, "query_grads", (shape(queries.shape, BF16),), (own, near, far, own_grads, near_grads, far_grads), 3 * flops)
    grad_keys, grad_values = call(add_kernel, "add", (shape(keys.shape, BF16), shape(values.shape, BF16)), (own_sums, near_back, far_back))
    return grad_queries, grad_keys, grad_values


def solution(mesh):
    placed = (
        P("section", "ctx", None),
        P("section", "ctx", None),
        P("section", "ctx", None),
        P("section", "ctx", None),
        P("section", None, "ctx"),
        P("section", "ctx", None),
        P("ctx"),
    )
    return jax.shard_map(
        per_device,
        mesh=mesh,
        in_specs=placed,
        out_specs=(P("section", "ctx", None), P("section", "ctx", None), P("section", "ctx", None)),
        check_vma=False,
    )
```

```python
import functools

import jax
import jax.numpy as jnp
from jax import lax
from jax.experimental import pallas as pl
from jax.experimental.pallas import tpu as pltpu
from jax.sharding import PartitionSpec as P

HOPS = 2
ORDERS = ((2, 1), (1, 2))
DOC_ROWS = 16
LAST_ROW = 8
COUNT_ROW = 9
FACT_ROWS = 8
NONE, FEW_KEYS, FEW_QUERIES, ALL = range(4)
BACK_STRIDE = 4
EARLY_HEADS = 6
LOG2_E = 1.4426950408889634
MASKED = -1e30

F32 = jnp.float32
BF16 = jnp.bfloat16


def from_behind(block, axis, distance):
    devices = range(lax.axis_size(axis))
    route = [((i - distance) % len(devices), i) for i in devices]
    return lax.ppermute(block, axis, route)


def full_routes(sections, shards, by, parity):
    route = {}
    for at in range(0, sections, 2):
        there, back = at + parity, at + 1 - parity
        for c in range(shards - by):
            route[there, c] = (there, c + by)
        free = set(range(shards))
        for last in range(shards - by, shards):
            first = last - shards + by
            way = [(there, last)] + [(back, c) for c in range(last, by - 1, -BACK_STRIDE)] + [(back, first), (there, first)]
            free -= {c for section, c in way if section == back}
            route.update(zip(way, way[1:]))
        for lane in range(BACK_STRIDE):
            rest = [c for c in sorted(free) if c % BACK_STRIDE == lane]
            pairs = [(c, c + 1) for c in rest if c + 1 in free] if by > 1 else []
            if by == 1:
                pairs = list(zip(rest[0::2], rest[1::2])) if len(rest) % 2 == 0 else []
                if not pairs:
                    route.update({(back, c): (back, rest[k - len(rest) + 1]) for k, c in enumerate(rest)})
            for c, d in pairs:
                route.update({(back, c): (back, d), (back, d): (back, c)})
    full = sections * shards
    whole = len(route) == full and len(set(route.values())) == full and all(a != b for a, b in route.items())
    return [(a * shards + c, b * shards + d) for (a, c), (b, d) in sorted(route.items())] if whole else None


def routes_behind(sections, shards, hop, parity):
    whole = sections % 2 == 0 and shards >= 4 * BACK_STRIDE
    route = full_routes(sections, shards, hop, parity) if whole else None
    if route is None:
        route = [(s * shards + c, s * shards + c + hop) for s in range(parity, sections, 2) for c in range(shards - hop)]
    return route


def returned(sums, order, ring):
    sections, shards = lax.axis_size("section"), lax.axis_size("ctx")
    hops = [order[s % 2] for s in range(sections)]
    pairs = [(s * shards + c, s * shards + (c - hops[s]) % shards) for s in range(sections) for c in range(0 if ring else hops[s], shards)]
    return lax.ppermute(sums, ("section", "ctx"), pairs)


def dot_nt(a, b):
    return lax.dot_general(a, b, (((1,), (1,)), ((), ())), preferred_element_type=F32)


def dot_nn(a, b):
    return lax.dot_general(a, b, (((1,), (0,)), ((), ())), preferred_element_type=F32)


def pack_kernel(keys, values, docs, packed, docs_here, sems):
    rows, width = keys.shape[1:]
    copies = [
        pltpu.make_async_copy(docs, docs_here, sems.at[0]),
        pltpu.make_async_copy(keys.at[0], packed.at[0:rows, 0:width], sems.at[1]),
        pltpu.make_async_copy(values.at[0], packed.at[0:rows, width : 2 * width], sems.at[2]),
    ]
    for copy in copies:
        copy.start()
    copies[0].wait()
    docs_row = docs_here[...]
    last = jnp.max(docs_row, axis=1, keepdims=True)
    last_count = jnp.sum((docs_row == last).astype(F32), axis=1, keepdims=True)
    row_at = lax.broadcasted_iota(jnp.int32, (DOC_ROWS, rows), 0)
    table = jnp.where(row_at == LAST_ROW, last.astype(F32) + 1, jnp.where(row_at == COUNT_ROW, last_count, docs_row.astype(F32) + 1))
    packed[rows : rows + DOC_ROWS, :] = table.astype(BF16)
    for copy in copies[1:]:
        copy.wait()


def column_of(row, width):
    rows = row.shape[1]
    column = jnp.transpose(jnp.broadcast_to(row, (width, rows)))
    return jnp.concatenate([column] * (rows // width), axis=1)


def block_grads(queries, grads, log_sums, delta_of, block, bias, score_grads, weights_low, sums, first_key, query_rows, chosen=None):
    rows = queries.shape[1]
    width = block.shape[1] // 2
    chosen = range(log_sums.shape[1]) if chosen is None else chosen
    scale = float(width) ** -0.5
    beside = rows // query_rows
    key_rows = slice(first_key, rows)
    side = lambda pieces: pieces[0] if len(pieces) == 1 else jnp.concatenate(pieces, axis=1)
    under = lambda pieces: pieces[0] if len(pieces) == 1 else jnp.concatenate(pieces, axis=0)
    part = lambda ref, head: ref[0, 0:query_rows, head * width : (head + 1) * width]
    columns = lambda head: slice(head * rows, head * rows + query_rows)
    masked = side([bias[key_rows, 0:query_rows]] * beside)
    for head in chosen[::beside]:
        group = range(head, head + beside)
        g = under([part(grads, h) for h in group])
        delta = side([delta_of(h, part(grads, h))[:, 0:query_rows] for h in group])
        lse = side([log_sums[0, h : h + 1, 0:query_rows] for h in group]) * LOG2_E
        scores = dot_nt(block[key_rows, 0:width], under([part(queries, h) for h in group]))
        weights = jnp.exp2(scores * (scale * LOG2_E) - lse + masked)
        weight_grads = dot_nt(block[key_rows, width : 2 * width], g)
        low = (weights * (weight_grads - delta)).astype(BF16)
        weights = weights.astype(BF16)
        for at, h in enumerate(group):
            here = slice(at * query_rows, (at + 1) * query_rows)
            score_grads[key_rows, columns(h)] = low[:, here]
            weights_low[key_rows, columns(h)] = weights[:, here]
    straight = slice(chosen[0] * rows, (chosen[-1] + 1) * rows)
    everything = lambda ref: ref[key_rows, straight] if beside == 1 else side([ref[key_rows, columns(h)] for h in chosen])
    stacked = lambda ref: under([part(ref, h) for h in chosen])
    sums[key_rows, 0:width] = (dot_nn(everything(score_grads), stacked(queries)) * scale).astype(sums.dtype)
    sums[key_rows, width : 2 * width] = dot_nn(everything(weights_low), stacked(grads)).astype(sums.dtype)


def own_bias(block, bias):
    rows = bias.shape[0]
    docs = block[rows : rows + DOC_ROWS, :].astype(F32)[0:1]
    key_at = lax.broadcasted_iota(jnp.int32, (rows, rows), 0)
    query_at = lax.broadcasted_iota(jnp.int32, (rows, rows), 1)
    bias[...] = jnp.where((column_of(docs, block.shape[1] // 2) == docs) & (key_at <= query_at), 0.0, MASKED)


def own_kernel(chosen, queries, attn_out, grads, log_sums, block, score_grads, sums, deltas, block_again, bias, weights_low):
    rows = queries.shape[1]
    heads = log_sums.shape[1]
    width = block.shape[1] // 2
    block_again[...] = block[...]
    docs = block[rows : rows + DOC_ROWS, :].astype(F32)[0:1]
    first_count = jnp.sum((docs == docs[:, 0:1]).astype(F32), axis=1, keepdims=True)
    deltas[heads:, :] = jnp.broadcast_to(first_count, (FACT_ROWS, rows))
    own_bias(block, bias)
    one = jnp.ones((8, width), BF16)
    for head in range(heads):
        part = slice(head * width, (head + 1) * width)
        product = grads[0, :, part].astype(F32) * attn_out[0, :, part].astype(F32)
        high = product.astype(BF16)
        low = (product - high.astype(F32)).astype(BF16)
        deltas[head : head + 1, :] = (dot_nt(one, high) + dot_nt(one, low))[0:1]
    delta_of = lambda head, g: deltas[head : head + 1, :]
    block_grads(queries, grads, log_sums, delta_of, block, bias, score_grads, weights_low, sums, 0, rows, chosen)


def rest_kernel(chosen, queries, grads, log_sums, deltas, block, before, first_grads, score_grads, sums, bias, weights_low):
    own_bias(block, bias)
    delta_of = lambda head, g: deltas[head : head + 1, :]
    block_grads(queries, grads, log_sums, delta_of, block, bias, score_grads, weights_low, sums, 0, queries.shape[1], chosen)


def hop_kernel(hop, parity, queries, grads, log_sums, deltas, own, block, before, *refs):
    score_grads, sums, bias, weights_low = refs[-4:]

    def reachable():
        rows = queries.shape[1]
        half = rows // 2
        docs = own[rows : rows + DOC_ROWS, :].astype(F32)[0:1]
        table = block[rows : rows + DOC_ROWS, :].astype(F32)
        same = (table[LAST_ROW : LAST_ROW + 1] == docs[:, 0:1]) & (lax.axis_index("ctx") >= hop)
        key_count = jnp.where(same, table[COUNT_ROW : COUNT_ROW + 1], 0.0)
        query_count = deltas[log_sums.shape[1] : log_sums.shape[1] + 1, :]
        key_at = lax.broadcasted_iota(jnp.int32, (rows, rows), 0).astype(F32)
        bias[...] = jnp.where((key_at >= rows - key_count) & (docs == docs[:, 0:1]), 0.0, MASKED)
        some = jnp.where(query_count <= half, FEW_QUERIES, ALL)
        mode = jnp.where(key_count == 0, NONE, jnp.where(key_count <= half, FEW_KEYS, some))[0, 0]
        delta_of = lambda head, g: deltas[head : head + 1, :]
        work = functools.partial(block_grads, queries, grads, log_sums, delta_of, block, bias, score_grads, weights_low, sums)

        @pl.when(mode == NONE)
        def _():
            score_grads[...] = jnp.zeros_like(score_grads)
            sums[...] = jnp.zeros_like(sums)

        @pl.when(mode == FEW_KEYS)
        def _():
            score_grads[0:half, :] = jnp.zeros((half, score_grads.shape[1]), BF16)
            sums[0:half, :] = jnp.zeros((half, sums.shape[1]), BF16)
            work(half, rows)

        @pl.when(mode == FEW_QUERIES)
        def _():
            for head in range(score_grads.shape[1] // rows):
                score_grads[:, head * rows + half : (head + 1) * rows] = jnp.zeros((rows, rows - half), BF16)
            work(0, half)

        if hop < HOPS:

            @pl.when(mode == ALL)
            def _():
                work(0, rows)

    pl.when(lax.axis_index("section") % 2 == parity)(reachable)


def pick(candidates, block):
    for parity, candidate in enumerate(candidates):

        @pl.when(lax.axis_index("section") % 2 == parity)
        def _():
            block[...] = candidate[...]


def query_kernel(own, own_grads, first_grads, second_grads, first_even, first_odd, second_even, second_odd, grad_queries, first, second):
    pick((first_even, first_odd), first)
    pick((second_even, second_odd), second)
    rows = own_grads.shape[0]
    heads = own_grads.shape[1] // rows
    width = own.shape[1] // 2
    scale = float(width) ** -0.5
    turned = [jnp.transpose(block[0:rows, 0:width].astype(F32)).astype(BF16) for block in (own, first, second)]
    for head in range(heads):
        columns = slice(head * rows, (head + 1) * rows)
        total = dot_nn(turned[0], own_grads[:, columns]) + dot_nn(turned[1], first_grads[:, columns]) + dot_nn(turned[2], second_grads[:, columns])
        grad_queries[0, :, head * width : (head + 1) * width] = jnp.transpose(total * scale).astype(BF16)


def add_kernel(shards, own_sums, rest_sums, first_sums, second_sums, grad_keys, grad_values):
    width = grad_keys.shape[2]
    total = own_sums[...] + rest_sums[...]
    for order, part in zip(ORDERS, (first_sums, second_sums)):
        hop = jnp.where(lax.axis_index("section") % 2 == 0, *order)
        total = total + jnp.where(lax.axis_index("ctx") + hop < shards, part[...].astype(F32), 0.0)
    grad_keys[0] = total[:, 0:width].astype(BF16)
    grad_values[0] = total[:, width : 2 * width].astype(BF16)


def call(kernel, name, outs, args, flops=0, scratch=(), from_hbm=0, kept=(), limit=8):
    args = [pltpu.with_memory_space_constraint(a, pltpu.HBM) for a in args[:from_hbm]] + list(args[from_hbm:])
    moved = sum(a.size * a.dtype.itemsize for a in args)
    vmem = lambda count: [pl.BlockSpec(memory_space=pltpu.VMEM)] * count
    return pl.pallas_call(
        kernel,
        out_shape=outs,
        in_specs=[pl.BlockSpec(memory_space=pltpu.HBM)] * from_hbm + vmem(len(args) - from_hbm + len(kept)),
        out_specs=tuple(vmem(len(outs))),
        scratch_shapes=list(scratch),
        input_output_aliases={len(args) + i: i for i in range(len(kept))},
        compiler_params=pltpu.CompilerParams(vmem_limit_bytes=limit * 1024 * 1024),
        cost_estimate=pl.CostEstimate(flops=flops, bytes_accessed=moved, transcendentals=0),
        name=name,
    )(*args, *kept)


def per_device(queries, keys, values, attn_out, log_sums, grad_held, doc_ids):
    rows, width = keys.shape[1:]
    heads = log_sums.shape[1]
    shape = jax.ShapeDtypeStruct
    flops = 2 * heads * rows * rows * width
    score_grads = shape((rows, heads * rows), BF16)
    scratch = [pltpu.VMEM((rows, rows), F32), pltpu.VMEM((rows, heads * rows), BF16)]
    sums = lambda dtype: shape((rows, 2 * width), dtype)

    grads = from_behind(grad_held, "section", -1)
    (own,) = call(
        pack_kernel,
        "pack",
        (shape((rows + DOC_ROWS, 2 * width), BF16),),
        (keys, values, doc_ids.reshape(1, rows)),
        40 * flops,
        [pltpu.VMEM((1, rows), jnp.int32), pltpu.SemaphoreType.DMA((3,))],
        3,
    )
    sections, shards = lax.axis_size("section"), lax.axis_size("ctx")
    behind = lambda block, order: [
        lax.ppermute(block, ("section", "ctx"), routes_behind(sections, shards, hop, parity)) for parity, hop in enumerate(order)
    ]
    first_order, second_order = ORDERS
    first = behind(own, first_order)
    early = range(EARLY_HEADS * heads // 8)
    late = range(len(early), heads)
    own_grads, own_sums, deltas, own_again = call(
        functools.partial(own_kernel, early),
        "own_block",
        (score_grads, sums(F32), shape((heads + FACT_ROWS, rows), F32), shape(own.shape, BF16)),
        (queries, attn_out, grads, log_sums, own),
        4 * flops,
        scratch,
    )
    second = behind(own_again, second_order)

    def block_of(name, order, before, candidates):
        kept = ()
        for parity, (hop, block) in enumerate(zip(order, candidates)):
            args = (queries, grads, log_sums, deltas, own, block, before)
            kept = call(functools.partial(hop_kernel, hop, parity), name, (score_grads, sums(BF16)), args, 4 * flops, scratch, 0, kept)
        return kept

    first_grads, first_sums = block_of("first_block", first_order, own_sums, first)
    first_back = returned(first_sums, first_order, True)
    second_grads, second_sums = block_of("second_block", second_order, first_sums, second)
    second_back = returned(second_sums, second_order, True)
    own_grads, rest_sums = call(
        functools.partial(rest_kernel, late),
        "own_rest",
        (score_grads, sums(F32)),
        (queries, grads, log_sums, deltas, own, second_sums),
        2 * flops,
        scratch,
        0,
        (own_grads,),
    )
    (grad_queries,) = call(
        query_kernel,
        "query_grads",
        (shape(queries.shape, BF16),),
        (own, own_grads, first_grads, second_grads, *first, *second),
        3 * flops,
        [pltpu.VMEM(own.shape, BF16)] * 2,
    )
    grad_keys, grad_values = call(
        functools.partial(add_kernel, shards), "add", (shape(keys.shape, BF16), shape(values.shape, BF16)), (own_sums, rest_sums, first_back, second_back)
    )
    return grad_queries, grad_keys, grad_values


def solution(mesh):
    placed = (
        P("section", "ctx", None),
        P("section", "ctx", None),
        P("section", "ctx", None),
        P("section", "ctx", None),
        P("section", None, "ctx"),
        P("section", "ctx", None),
        P("ctx"),
    )
    return jax.shard_map(
        per_device,
        mesh=mesh,
        in_specs=placed,
        out_specs=(P("section", "ctx", None), P("section", "ctx", None), P("section", "ctx", None)),
        check_vma=False,
    )
```

```python
import functools

import jax
import jax.numpy as jnp
from jax import lax
from jax.experimental import pallas as pl
from jax.experimental.pallas import tpu as pltpu
from jax.sharding import PartitionSpec as P

HOPS = 2
ORDERS = ((2, 1), (1, 2))
DOC_ROWS = 16
LAST_ROW = 8
COUNT_ROW = 9
FACT_ROWS = 8
NONE, FEW_KEYS, FEW_QUERIES, ALL = range(4)
BACK_STRIDE = 4
EARLY_HEADS = 4
LOG2_E = 1.4426950408889634
MASKED = -1e30

F32 = jnp.float32
BF16 = jnp.bfloat16


def from_behind(block, axis, distance):
    devices = range(lax.axis_size(axis))
    route = [((i - distance) % len(devices), i) for i in devices]
    return lax.ppermute(block, axis, route)


def full_routes(sections, shards, by, parity):
    route = {}
    for at in range(0, sections, 2):
        there, back = at + parity, at + 1 - parity
        for c in range(shards - by):
            route[there, c] = (there, c + by)
        free = set(range(shards))
        for last in range(shards - by, shards):
            first = last - shards + by
            way = [(there, last)] + [(back, c) for c in range(last, by - 1, -BACK_STRIDE)] + [(back, first), (there, first)]
            free -= {c for section, c in way if section == back}
            route.update(zip(way, way[1:]))
        for lane in range(BACK_STRIDE):
            rest = [c for c in sorted(free) if c % BACK_STRIDE == lane]
            pairs = [(c, c + 1) for c in rest if c + 1 in free] if by > 1 else []
            if by == 1:
                pairs = list(zip(rest[0::2], rest[1::2])) if len(rest) % 2 == 0 else []
                if not pairs:
                    route.update({(back, c): (back, rest[k - len(rest) + 1]) for k, c in enumerate(rest)})
            for c, d in pairs:
                route.update({(back, c): (back, d), (back, d): (back, c)})
    full = sections * shards
    whole = len(route) == full and len(set(route.values())) == full and all(a != b for a, b in route.items())
    return [(a * shards + c, b * shards + d) for (a, c), (b, d) in sorted(route.items())] if whole else None


def routes_behind(sections, shards, hop, parity):
    whole = sections % 2 == 0 and shards >= 4 * BACK_STRIDE
    route = full_routes(sections, shards, hop, parity) if whole else None
    if route is None:
        route = [(s * shards + c, s * shards + c + hop) for s in range(parity, sections, 2) for c in range(shards - hop)]
    return route


def returned(sums, order):
    sections, shards = lax.axis_size("section"), lax.axis_size("ctx")
    hop_of = lambda section: order[section % 2]
    route = {(s, c): (s, c - hop_of(s)) for s in range(sections) for c in range(hop_of(s), shards)}
    idle = [(s, c) for s in range(sections) for c in range(shards - hop_of(s), shards)]
    for s in range(sections):
        for c in range(hop_of(s)):
            route[s, c] = min(idle, key=lambda there: ((there[1] - c) % 2, abs(there[0] - s)))
            idle.remove(route[s, c])
    return lax.ppermute(sums, ("section", "ctx"), [(s * shards + c, t * shards + d) for (s, c), (t, d) in route.items()])


def dot_nt(a, b):
    return lax.dot_general(a, b, (((1,), (1,)), ((), ())), preferred_element_type=F32)


def dot_nn(a, b):
    return lax.dot_general(a, b, (((1,), (0,)), ((), ())), preferred_element_type=F32)


def pack_kernel(keys, values, docs, packed, docs_here, sems):
    rows, width = keys.shape[1:]
    copies = [
        pltpu.make_async_copy(docs, docs_here, sems.at[0]),
        pltpu.make_async_copy(keys.at[0], packed.at[0:rows, 0:width], sems.at[1]),
        pltpu.make_async_copy(values.at[0], packed.at[0:rows, width : 2 * width], sems.at[2]),
    ]
    for copy in copies:
        copy.start()
    copies[0].wait()
    docs_row = docs_here[...]
    last = jnp.max(docs_row, axis=1, keepdims=True)
    last_count = jnp.sum((docs_row == last).astype(F32), axis=1, keepdims=True)
    row_at = lax.broadcasted_iota(jnp.int32, (DOC_ROWS, rows), 0)
    table = jnp.where(row_at == LAST_ROW, last.astype(F32) + 1, jnp.where(row_at == COUNT_ROW, last_count, docs_row.astype(F32) + 1))
    packed[rows : rows + DOC_ROWS, :] = table.astype(BF16)
    for copy in copies[1:]:
        copy.wait()


def column_of(row, width):
    rows = row.shape[1]
    column = jnp.transpose(jnp.broadcast_to(row, (width, rows)))
    return jnp.concatenate([column] * (rows // width), axis=1)


def block_grads(queries, grads, log_sums, delta_of, block, bias, score_grads, weights_low, sums, first_key, query_rows, chosen=None):
    rows = queries.shape[1]
    width = block.shape[1] // 2
    chosen = range(log_sums.shape[1]) if chosen is None else chosen
    scale = float(width) ** -0.5
    beside = rows // query_rows
    key_rows = slice(first_key, rows)
    side = lambda pieces: pieces[0] if len(pieces) == 1 else jnp.concatenate(pieces, axis=1)
    under = lambda pieces: pieces[0] if len(pieces) == 1 else jnp.concatenate(pieces, axis=0)
    part = lambda ref, head: ref[0, 0:query_rows, head * width : (head + 1) * width]
    columns = lambda head: slice(head * rows, head * rows + query_rows)
    masked = side([bias[key_rows, 0:query_rows]] * beside)
    for head in chosen[::beside]:
        group = range(head, head + beside)
        g = under([part(grads, h) for h in group])
        delta = side([delta_of(h, part(grads, h))[:, 0:query_rows] for h in group])
        lse = side([log_sums[0, h : h + 1, 0:query_rows] for h in group]) * LOG2_E
        scores = dot_nt(block[key_rows, 0:width], under([part(queries, h) for h in group]))
        weights = jnp.exp2(scores * (scale * LOG2_E) - lse + masked)
        weight_grads = dot_nt(block[key_rows, width : 2 * width], g)
        low = (weights * (weight_grads - delta)).astype(BF16)
        weights = weights.astype(BF16)
        for at, h in enumerate(group):
            here = slice(at * query_rows, (at + 1) * query_rows)
            score_grads[key_rows, columns(h)] = low[:, here]
            weights_low[key_rows, columns(h)] = weights[:, here]
    straight = slice(chosen[0] * rows, (chosen[-1] + 1) * rows)
    everything = lambda ref: ref[key_rows, straight] if beside == 1 else side([ref[key_rows, columns(h)] for h in chosen])
    stacked = lambda ref: under([part(ref, h) for h in chosen])
    sums[key_rows, 0:width] = (dot_nn(everything(score_grads), stacked(queries)) * scale).astype(sums.dtype)
    sums[key_rows, width : 2 * width] = dot_nn(everything(weights_low), stacked(grads)).astype(sums.dtype)


def own_bias(block, bias):
    rows = bias.shape[0]
    docs = block[rows : rows + DOC_ROWS, :].astype(F32)[0:1]
    key_at = lax.broadcasted_iota(jnp.int32, (rows, rows), 0)
    query_at = lax.broadcasted_iota(jnp.int32, (rows, rows), 1)
    bias[...] = jnp.where((column_of(docs, block.shape[1] // 2) == docs) & (key_at <= query_at), 0.0, MASKED)


def own_kernel(chosen, queries, attn_out, grads, log_sums, block, score_grads, sums, deltas, block_again, bias, weights_low):
    rows = queries.shape[1]
    heads = log_sums.shape[1]
    width = block.shape[1] // 2
    block_again[...] = block[...]
    docs = block[rows : rows + DOC_ROWS, :].astype(F32)[0:1]
    first_count = jnp.sum((docs == docs[:, 0:1]).astype(F32), axis=1, keepdims=True)
    deltas[heads:, :] = jnp.broadcast_to(first_count, (FACT_ROWS, rows))
    own_bias(block, bias)
    one = jnp.ones((8, width), BF16)
    for head in range(heads):
        part = slice(head * width, (head + 1) * width)
        product = grads[0, :, part].astype(F32) * attn_out[0, :, part].astype(F32)
        high = product.astype(BF16)
        low = (product - high.astype(F32)).astype(BF16)
        deltas[head : head + 1, :] = (dot_nt(one, high) + dot_nt(one, low))[0:1]
    delta_of = lambda head, g: deltas[head : head + 1, :]
    block_grads(queries, grads, log_sums, delta_of, block, bias, score_grads, weights_low, sums, 0, rows, chosen)


def rest_kernel(chosen, queries, grads, log_sums, deltas, block, before, first_grads, score_grads, sums, bias, weights_low):
    own_bias(block, bias)
    delta_of = lambda head, g: deltas[head : head + 1, :]
    block_grads(queries, grads, log_sums, delta_of, block, bias, score_grads, weights_low, sums, 0, queries.shape[1], chosen)


def hop_kernel(hop, parity, queries, grads, log_sums, deltas, own, block, before, *refs):
    score_grads, sums, bias, weights_low = refs[-4:]

    def reachable():
        rows = queries.shape[1]
        half = rows // 2
        docs = own[rows : rows + DOC_ROWS, :].astype(F32)[0:1]
        table = block[rows : rows + DOC_ROWS, :].astype(F32)
        same = (table[LAST_ROW : LAST_ROW + 1] == docs[:, 0:1]) & (lax.axis_index("ctx") >= hop)
        key_count = jnp.where(same, table[COUNT_ROW : COUNT_ROW + 1], 0.0)
        query_count = deltas[log_sums.shape[1] : log_sums.shape[1] + 1, :]
        key_at = lax.broadcasted_iota(jnp.int32, (rows, rows), 0).astype(F32)
        bias[...] = jnp.where((key_at >= rows - key_count) & (docs == docs[:, 0:1]), 0.0, MASKED)
        some = jnp.where(query_count <= half, FEW_QUERIES, ALL)
        mode = jnp.where(key_count == 0, NONE, jnp.where(key_count <= half, FEW_KEYS, some))[0, 0]
        delta_of = lambda head, g: deltas[head : head + 1, :]
        work = functools.partial(block_grads, queries, grads, log_sums, delta_of, block, bias, score_grads, weights_low, sums)

        @pl.when(mode == NONE)
        def _():
            score_grads[...] = jnp.zeros_like(score_grads)
            sums[...] = jnp.zeros_like(sums)

        @pl.when(mode == FEW_KEYS)
        def _():
            score_grads[0:half, :] = jnp.zeros((half, score_grads.shape[1]), BF16)
            sums[0:half, :] = jnp.zeros((half, sums.shape[1]), BF16)
            work(half, rows)

        @pl.when(mode == FEW_QUERIES)
        def _():
            for head in range(score_grads.shape[1] // rows):
                score_grads[:, head * rows + half : (head + 1) * rows] = jnp.zeros((rows, rows - half), BF16)
            work(0, half)

        if hop < HOPS:

            @pl.when(mode == ALL)
            def _():
                work(0, rows)

    pl.when(lax.axis_index("section") % 2 == parity)(reachable)


def pick(candidates, block):
    for parity, candidate in enumerate(candidates):

        @pl.when(lax.axis_index("section") % 2 == parity)
        def _():
            block[...] = candidate[...]


def query_kernel(own, own_grads, first_grads, second_grads, first_even, first_odd, second_even, second_odd, grad_queries, first, second):
    pick((first_even, first_odd), first)
    pick((second_even, second_odd), second)
    rows = own_grads.shape[0]
    heads = own_grads.shape[1] // rows
    width = own.shape[1] // 2
    scale = float(width) ** -0.5
    turned = [jnp.transpose(block[0:rows, 0:width].astype(F32)).astype(BF16) for block in (own, first, second)]
    for head in range(heads):
        columns = slice(head * rows, (head + 1) * rows)
        total = dot_nn(turned[0], own_grads[:, columns]) + dot_nn(turned[1], first_grads[:, columns]) + dot_nn(turned[2], second_grads[:, columns])
        grad_queries[0, :, head * width : (head + 1) * width] = jnp.transpose(total * scale).astype(BF16)


def add_kernel(shards, own_sums, rest_sums, first_sums, second_sums, grad_keys, grad_values):
    width = grad_keys.shape[2]
    total = own_sums[...] + rest_sums[...]
    for order, part in zip(ORDERS, (first_sums, second_sums)):
        hop = jnp.where(lax.axis_index("section") % 2 == 0, *order)
        total = total + jnp.where(lax.axis_index("ctx") + hop < shards, part[...].astype(F32), 0.0)
    grad_keys[0] = total[:, 0:width].astype(BF16)
    grad_values[0] = total[:, width : 2 * width].astype(BF16)


def call(kernel, name, outs, args, flops=0, scratch=(), from_hbm=0, kept=(), limit=8):
    args = [pltpu.with_memory_space_constraint(a, pltpu.HBM) for a in args[:from_hbm]] + list(args[from_hbm:])
    moved = sum(a.size * a.dtype.itemsize for a in args)
    vmem = lambda count: [pl.BlockSpec(memory_space=pltpu.VMEM)] * count
    return pl.pallas_call(
        kernel,
        out_shape=outs,
        in_specs=[pl.BlockSpec(memory_space=pltpu.HBM)] * from_hbm + vmem(len(args) - from_hbm + len(kept)),
        out_specs=tuple(vmem(len(outs))),
        scratch_shapes=list(scratch),
        input_output_aliases={len(args) + i: i for i in range(len(kept))},
        compiler_params=pltpu.CompilerParams(vmem_limit_bytes=limit * 1024 * 1024),
        cost_estimate=pl.CostEstimate(flops=flops, bytes_accessed=moved, transcendentals=0),
        name=name,
    )(*args, *kept)


def per_device(queries, keys, values, attn_out, log_sums, grad_held, doc_ids):
    rows, width = keys.shape[1:]
    heads = log_sums.shape[1]
    shape = jax.ShapeDtypeStruct
    flops = 2 * heads * rows * rows * width
    score_grads = shape((rows, heads * rows), BF16)
    scratch = [pltpu.VMEM((rows, rows), F32), pltpu.VMEM((rows, heads * rows), BF16)]
    sums = lambda dtype: shape((rows, 2 * width), dtype)

    grads = from_behind(grad_held, "section", -1)
    (own,) = call(
        pack_kernel,
        "pack",
        (shape((rows + DOC_ROWS, 2 * width), BF16),),
        (keys, values, doc_ids.reshape(1, rows)),
        40 * flops,
        [pltpu.VMEM((1, rows), jnp.int32), pltpu.SemaphoreType.DMA((3,))],
        3,
    )
    sections, shards = lax.axis_size("section"), lax.axis_size("ctx")
    behind = lambda block, order: [
        lax.ppermute(block, ("section", "ctx"), routes_behind(sections, shards, hop, parity)) for parity, hop in enumerate(order)
    ]
    first_order, second_order = ORDERS
    first = behind(own, first_order)
    early = range(EARLY_HEADS * heads // 8)
    late = range(len(early), heads)
    own_grads, own_sums, deltas, own_again = call(
        functools.partial(own_kernel, early),
        "own_block",
        (score_grads, sums(F32), shape((heads + FACT_ROWS, rows), F32), shape(own.shape, BF16)),
        (queries, attn_out, grads, log_sums, own),
        4 * flops,
        scratch,
    )
    second = behind(own_again, second_order)

    def block_of(name, order, before, candidates):
        kept = ()
        for parity, (hop, block) in enumerate(zip(order, candidates)):
            args = (queries, grads, log_sums, deltas, own, block, before)
            kept = call(functools.partial(hop_kernel, hop, parity), name, (score_grads, sums(BF16)), args, 4 * flops, scratch, 0, kept)
        return kept

    first_grads, first_sums = block_of("first_block", first_order, own_sums, first)
    first_back = returned(first_sums, first_order)
    second_grads, second_sums = block_of("second_block", second_order, first_sums, second)
    second_back = returned(second_sums, second_order)
    own_grads, rest_sums = call(
        functools.partial(rest_kernel, late),
        "own_rest",
        (score_grads, sums(F32)),
        (queries, grads, log_sums, deltas, own, second_sums),
        2 * flops,
        scratch,
        0,
        (own_grads,),
    )
    (grad_queries,) = call(
        query_kernel,
        "query_grads",
        (shape(queries.shape, BF16),),
        (own, own_grads, first_grads, second_grads, *first, *second),
        3 * flops,
        [pltpu.VMEM(own.shape, BF16)] * 2,
    )
    grad_keys, grad_values = call(
        functools.partial(add_kernel, shards), "add", (shape(keys.shape, BF16), shape(values.shape, BF16)), (own_sums, rest_sums, first_back, second_back)
    )
    return grad_queries, grad_keys, grad_values


def solution(mesh):
    placed = (
        P("section", "ctx", None),
        P("section", "ctx", None),
        P("section", "ctx", None),
        P("section", "ctx", None),
        P("section", None, "ctx"),
        P("section", "ctx", None),
        P("ctx"),
    )
    return jax.shard_map(
        per_device,
        mesh=mesh,
        in_specs=placed,
        out_specs=(P("section", "ctx", None), P("section", "ctx", None), P("section", "ctx", None)),
        check_vma=False,
    )
```

```python
import functools

import jax
import jax.numpy as jnp
from jax import lax
from jax.experimental import pallas as pl
from jax.experimental.pallas import tpu as pltpu
from jax.sharding import PartitionSpec as P

HOPS = 2
ORDERS = ((2, 1), (1, 2))
TABLE_ROWS = 16
LAST_ROW = 0
COUNT_ROW = 8
FACT_ROWS = 8
NONE, FEW_KEYS, FEW_QUERIES, ALL = range(4)
BACK_STRIDE = 4
EARLY_HEADS = 4
LOG2_E = 1.4426950408889634
MASKED = -1e30

F32 = jnp.float32
BF16 = jnp.bfloat16


def from_behind(block, axis, distance):
    devices = range(lax.axis_size(axis))
    route = [((i - distance) % len(devices), i) for i in devices]
    return lax.ppermute(block, axis, route)


def full_routes(sections, shards, by, parity):
    route = {}
    for at in range(0, sections, 2):
        there, back = at + parity, at + 1 - parity
        for c in range(shards - by):
            route[there, c] = (there, c + by)
        free = set(range(shards))
        for last in range(shards - by, shards):
            first = last - shards + by
            way = [(there, last)] + [(back, c) for c in range(last, by - 1, -BACK_STRIDE)] + [(back, first), (there, first)]
            free -= {c for section, c in way if section == back}
            route.update(zip(way, way[1:]))
        for lane in range(BACK_STRIDE):
            rest = [c for c in sorted(free) if c % BACK_STRIDE == lane]
            pairs = [(c, c + 1) for c in rest if c + 1 in free] if by > 1 else []
            if by == 1:
                pairs = list(zip(rest[0::2], rest[1::2])) if len(rest) % 2 == 0 else []
                if not pairs:
                    route.update({(back, c): (back, rest[k - len(rest) + 1]) for k, c in enumerate(rest)})
            for c, d in pairs:
                route.update({(back, c): (back, d), (back, d): (back, c)})
    full = sections * shards
    whole = len(route) == full and len(set(route.values())) == full and all(a != b for a, b in route.items())
    return [(a * shards + c, b * shards + d) for (a, c), (b, d) in sorted(route.items())] if whole else None


def routes_behind(sections, shards, hop, parity):
    whole = sections % 2 == 0 and shards >= 4 * BACK_STRIDE
    route = full_routes(sections, shards, hop, parity) if whole else None
    if route is None:
        route = [(s * shards + c, s * shards + c + hop) for s in range(parity, sections, 2) for c in range(shards - hop)]
    return route


def returned(sums, order):
    sections, shards = lax.axis_size("section"), lax.axis_size("ctx")
    hop_of = lambda section: order[section % 2]
    route = {(s, c): (s, c - hop_of(s)) for s in range(sections) for c in range(hop_of(s), shards)}
    idle = [(s, c) for s in range(sections) for c in range(shards - hop_of(s), shards)]
    for s in range(sections):
        for c in range(hop_of(s)):
            route[s, c] = min(idle, key=lambda there: ((there[1] - c) % 2, abs(there[0] - s)))
            idle.remove(route[s, c])
    return lax.ppermute(sums, ("section", "ctx"), [(s * shards + c, t * shards + d) for (s, c), (t, d) in route.items()])


def dot_nt(a, b):
    return lax.dot_general(a, b, (((1,), (1,)), ((), ())), preferred_element_type=F32)


def dot_nn(a, b):
    return lax.dot_general(a, b, (((1,), (0,)), ((), ())), preferred_element_type=F32)


def pack_kernel(keys, values, docs, packed, docs_row, docs_here, sems):
    rows, width = keys.shape[1:]
    copies = [
        pltpu.make_async_copy(docs, docs_here, sems.at[0]),
        pltpu.make_async_copy(keys.at[0], packed.at[0:rows, :], sems.at[1]),
        pltpu.make_async_copy(values.at[0], packed.at[rows : 2 * rows, :], sems.at[2]),
    ]
    for copy in copies:
        copy.start()
    copies[0].wait()
    numbers = docs_here[...]
    last = jnp.max(numbers, axis=1, keepdims=True)
    last_count = jnp.sum((numbers == last).astype(F32), axis=1, keepdims=True)
    row_at = lax.broadcasted_iota(jnp.int32, (TABLE_ROWS, width), 0)
    table = jnp.where(row_at == COUNT_ROW, last_count, last.astype(F32) + 1)
    packed[2 * rows : 2 * rows + TABLE_ROWS, :] = table.astype(BF16)
    docs_row[...] = jnp.broadcast_to(numbers.astype(F32) + 1, docs_row.shape)
    for copy in copies[1:]:
        copy.wait()


def column_of(row, width):
    rows = row.shape[1]
    column = jnp.transpose(jnp.broadcast_to(row, (width, rows)))
    return jnp.concatenate([column] * (rows // width), axis=1)


def block_grads(queries, grads, log_sums, delta_of, block, bias, score_grads, weights_low, sums, first_key, query_rows, chosen=None):
    rows = queries.shape[1]
    width = block.shape[1]
    chosen = range(log_sums.shape[1]) if chosen is None else chosen
    scale = float(width) ** -0.5
    beside = rows // query_rows
    key_rows = slice(first_key, rows)
    side = lambda pieces: pieces[0] if len(pieces) == 1 else jnp.concatenate(pieces, axis=1)
    under = lambda pieces: pieces[0] if len(pieces) == 1 else jnp.concatenate(pieces, axis=0)
    part = lambda ref, head: ref[0, 0:query_rows, head * width : (head + 1) * width]
    columns = lambda head: slice(head * rows, head * rows + query_rows)
    masked = side([bias[key_rows, 0:query_rows]] * beside)
    for head in chosen[::beside]:
        group = range(head, head + beside)
        g = under([part(grads, h) for h in group])
        delta = side([delta_of(h, part(grads, h))[:, 0:query_rows] for h in group])
        lse = side([log_sums[0, h : h + 1, 0:query_rows] for h in group]) * LOG2_E
        scores = dot_nt(block[key_rows, :], under([part(queries, h) for h in group]))
        weights = jnp.exp2(scores * (scale * LOG2_E) - lse + masked)
        weight_grads = dot_nt(block[rows + first_key : 2 * rows, :], g)
        low = (weights * (weight_grads - delta)).astype(BF16)
        weights = weights.astype(BF16)
        for at, h in enumerate(group):
            here = slice(at * query_rows, (at + 1) * query_rows)
            score_grads[key_rows, columns(h)] = low[:, here]
            weights_low[key_rows, columns(h)] = weights[:, here]
    straight = slice(chosen[0] * rows, (chosen[-1] + 1) * rows)
    everything = lambda ref: ref[key_rows, straight] if beside == 1 else side([ref[key_rows, columns(h)] for h in chosen])
    stacked = lambda ref: under([part(ref, h) for h in chosen])
    sums[key_rows, 0:width] = (dot_nn(everything(score_grads), stacked(queries)) * scale).astype(sums.dtype)
    sums[key_rows, width : 2 * width] = dot_nn(everything(weights_low), stacked(grads)).astype(sums.dtype)


def own_bias(docs_row, width, bias):
    rows = bias.shape[0]
    docs = docs_row[0:1, :]
    key_at = lax.broadcasted_iota(jnp.int32, (rows, rows), 0)
    query_at = lax.broadcasted_iota(jnp.int32, (rows, rows), 1)
    bias[...] = jnp.where((column_of(docs, width) == docs) & (key_at <= query_at), 0.0, MASKED)


def own_kernel(chosen, queries, attn_out, grads, log_sums, docs_row, block, score_grads, sums, deltas, block_again, bias, weights_low):
    rows = queries.shape[1]
    heads = log_sums.shape[1]
    width = block.shape[1]
    block_again[...] = block[...]
    docs = docs_row[0:1, :]
    first_count = jnp.sum((docs == docs[:, 0:1]).astype(F32), axis=1, keepdims=True)
    deltas[heads:, :] = jnp.broadcast_to(first_count, (FACT_ROWS, rows))
    own_bias(docs_row, width, bias)
    one = jnp.ones((8, width), BF16)
    for head in range(heads):
        part = slice(head * width, (head + 1) * width)
        product = grads[0, :, part].astype(F32) * attn_out[0, :, part].astype(F32)
        high = product.astype(BF16)
        low = (product - high.astype(F32)).astype(BF16)
        deltas[head : head + 1, :] = (dot_nt(one, high) + dot_nt(one, low))[0:1]
    delta_of = lambda head, g: deltas[head : head + 1, :]
    block_grads(queries, grads, log_sums, delta_of, block, bias, score_grads, weights_low, sums, 0, rows, chosen)


def rest_kernel(chosen, queries, grads, log_sums, docs_row, deltas, block, before, first_grads, score_grads, sums, bias, weights_low):
    own_bias(docs_row, block.shape[1], bias)
    delta_of = lambda head, g: deltas[head : head + 1, :]
    block_grads(queries, grads, log_sums, delta_of, block, bias, score_grads, weights_low, sums, 0, queries.shape[1], chosen)


def hop_kernel(hop, parity, queries, grads, log_sums, docs_row, deltas, block, before, *refs):
    score_grads, sums, bias, weights_low = refs[-4:]

    def reachable():
        rows = queries.shape[1]
        half = rows // 2
        docs = docs_row[0:1, :]
        table = block[2 * rows : 2 * rows + TABLE_ROWS, :].astype(F32)
        same = (table[LAST_ROW : LAST_ROW + 1, 0:1] == docs[:, 0:1]) & (lax.axis_index("ctx") >= hop)
        key_count = jnp.where(same, table[COUNT_ROW : COUNT_ROW + 1, 0:1], 0.0)
        query_count = deltas[log_sums.shape[1] : log_sums.shape[1] + 1, 0:1]
        key_at = lax.broadcasted_iota(jnp.int32, (rows, rows), 0).astype(F32)
        bias[...] = jnp.where((key_at >= rows - key_count) & (docs == docs[:, 0:1]), 0.0, MASKED)
        some = jnp.where(query_count <= half, FEW_QUERIES, ALL)
        mode = jnp.where(key_count == 0, NONE, jnp.where(key_count <= half, FEW_KEYS, some))[0, 0]
        delta_of = lambda head, g: deltas[head : head + 1, :]
        work = functools.partial(block_grads, queries, grads, log_sums, delta_of, block, bias, score_grads, weights_low, sums)

        @pl.when(mode == NONE)
        def _():
            score_grads[...] = jnp.zeros_like(score_grads)
            sums[...] = jnp.zeros_like(sums)

        @pl.when(mode == FEW_KEYS)
        def _():
            score_grads[0:half, :] = jnp.zeros((half, score_grads.shape[1]), BF16)
            sums[0:half, :] = jnp.zeros((half, sums.shape[1]), BF16)
            work(half, rows)

        @pl.when(mode == FEW_QUERIES)
        def _():
            for head in range(score_grads.shape[1] // rows):
                score_grads[:, head * rows + half : (head + 1) * rows] = jnp.zeros((rows, rows - half), BF16)
            work(0, half)

        if hop < HOPS:

            @pl.when(mode == ALL)
            def _():
                work(0, rows)

    pl.when(lax.axis_index("section") % 2 == parity)(reachable)


def pick(candidates, block):
    for parity, candidate in enumerate(candidates):

        @pl.when(lax.axis_index("section") % 2 == parity)
        def _():
            block[...] = candidate[...]


def query_kernel(own, own_grads, first_grads, second_grads, first_even, first_odd, second_even, second_odd, grad_queries, first, second):
    pick((first_even, first_odd), first)
    pick((second_even, second_odd), second)
    rows = own_grads.shape[0]
    heads = own_grads.shape[1] // rows
    width = own.shape[1]
    scale = float(width) ** -0.5
    turned = [jnp.transpose(block[0:rows, :].astype(F32)).astype(BF16) for block in (own, first, second)]
    for head in range(heads):
        columns = slice(head * rows, (head + 1) * rows)
        total = dot_nn(turned[0], own_grads[:, columns]) + dot_nn(turned[1], first_grads[:, columns]) + dot_nn(turned[2], second_grads[:, columns])
        grad_queries[0, :, head * width : (head + 1) * width] = jnp.transpose(total * scale).astype(BF16)


def reached(order, shards):
    hop = jnp.where(lax.axis_index("section") % 2 == 0, *order)
    return lax.axis_index("ctx") + hop < shards


def fold_kernel(shards, own_sums, rest_sums, first_sums, total):
    total[...] = own_sums[...] + rest_sums[...]

    @pl.when(reached(ORDERS[0], shards))
    def _():
        total[...] += first_sums[...].astype(F32)


def add_kernel(shards, folded, second_sums, grad_keys, grad_values, low, sems):
    rows, width = grad_keys.shape[1:]
    there = reached(ORDERS[1], shards).astype(F32)
    copies = []
    for at, target in enumerate((grad_keys, grad_values)):
        half = slice(at * width, (at + 1) * width)
        low[at] = (folded[:, half] + second_sums[:, half].astype(F32) * there).astype(BF16)
        copies.append(pltpu.make_async_copy(low.at[at], target.at[0], sems.at[at]))
        copies[-1].start()
    for copy in copies:
        copy.wait()


def call(kernel, name, outs, args, flops=0, scratch=(), from_hbm=0, kept=(), limit=8, to_hbm=False):
    args = [pltpu.with_memory_space_constraint(a, pltpu.HBM) for a in args[:from_hbm]] + list(args[from_hbm:])
    moved = sum(a.size * a.dtype.itemsize for a in args)
    vmem = lambda count: [pl.BlockSpec(memory_space=pltpu.VMEM)] * count
    return pl.pallas_call(
        kernel,
        out_shape=outs,
        in_specs=[pl.BlockSpec(memory_space=pltpu.HBM)] * from_hbm + vmem(len(args) - from_hbm + len(kept)),
        out_specs=tuple([pl.BlockSpec(memory_space=pltpu.HBM)] * len(outs) if to_hbm else vmem(len(outs))),
        scratch_shapes=list(scratch),
        input_output_aliases={len(args) + i: i for i in range(len(kept))},
        compiler_params=pltpu.CompilerParams(vmem_limit_bytes=limit * 1024 * 1024),
        cost_estimate=pl.CostEstimate(flops=flops, bytes_accessed=moved, transcendentals=0),
        name=name,
    )(*args, *kept)


def per_device(queries, keys, values, attn_out, log_sums, grad_held, doc_ids):
    rows, width = keys.shape[1:]
    heads = log_sums.shape[1]
    shape = jax.ShapeDtypeStruct
    flops = 2 * heads * rows * rows * width
    score_grads = shape((rows, heads * rows), BF16)
    scratch = [pltpu.VMEM((rows, rows), F32), pltpu.VMEM((rows, heads * rows), BF16)]
    sums = lambda dtype: shape((rows, 2 * width), dtype)

    grads = from_behind(grad_held, "section", -1)
    own, docs_row = call(
        pack_kernel,
        "pack",
        (shape((2 * rows + TABLE_ROWS, width), BF16), shape((8, rows), F32)),
        (keys, values, doc_ids.reshape(1, rows)),
        40 * flops,
        [pltpu.VMEM((1, rows), jnp.int32), pltpu.SemaphoreType.DMA((3,))],
        3,
    )
    sections, shards = lax.axis_size("section"), lax.axis_size("ctx")
    behind = lambda block, order: [
        lax.ppermute(block, ("section", "ctx"), routes_behind(sections, shards, hop, parity)) for parity, hop in enumerate(order)
    ]
    first_order, second_order = ORDERS
    first = behind(own, first_order)
    early = range(EARLY_HEADS * heads // 8)
    late = range(len(early), heads)
    own_grads, own_sums, deltas, own_again = call(
        functools.partial(own_kernel, early),
        "own_block",
        (score_grads, sums(F32), shape((heads + FACT_ROWS, rows), F32), shape(own.shape, BF16)),
        (queries, attn_out, grads, log_sums, docs_row, own),
        4 * flops,
        scratch,
    )
    second = behind(own_again, second_order)

    def block_of(name, order, before, candidates):
        kept = ()
        for parity, (hop, block) in enumerate(zip(order, candidates)):
            args = (queries, grads, log_sums, docs_row, deltas, block, before)
            kept = call(functools.partial(hop_kernel, hop, parity), name, (score_grads, sums(BF16)), args, 4 * flops, scratch, 0, kept)
        return kept

    first_grads, first_sums = block_of("first_block", first_order, own_sums, first)
    first_back = returned(first_sums, first_order)
    second_grads, second_sums = block_of("second_block", second_order, first_sums, second)
    second_back = returned(second_sums, second_order)
    own_grads, rest_sums = call(
        functools.partial(rest_kernel, late),
        "own_rest",
        (score_grads, sums(F32)),
        (queries, grads, log_sums, docs_row, deltas, own, second_sums),
        2 * flops,
        scratch,
        0,
        (own_grads,),
    )
    (grad_queries,) = call(
        query_kernel,
        "query_grads",
        (shape(queries.shape, BF16),),
        (own, own_grads, first_grads, second_grads, *first, *second),
        3 * flops,
        [pltpu.VMEM(own.shape, BF16)] * 2,
    )
    (folded,) = call(functools.partial(fold_kernel, shards), "fold", (sums(F32),), (own_sums, rest_sums, first_back))
    grad_keys, grad_values = call(
        functools.partial(add_kernel, shards),
        "add",
        (shape(keys.shape, BF16), shape(values.shape, BF16)),
        (folded, second_back),
        0,
        [pltpu.VMEM((2, rows, width), BF16), pltpu.SemaphoreType.DMA((2,))],
        to_hbm=True,
    )
    return grad_queries, grad_keys, grad_values


def solution(mesh):
    placed = (
        P("section", "ctx", None),
        P("section", "ctx", None),
        P("section", "ctx", None),
        P("section", "ctx", None),
        P("section", None, "ctx"),
        P("section", "ctx", None),
        P("ctx"),
    )
    return jax.shard_map(
        per_device,
        mesh=mesh,
        in_specs=placed,
        out_specs=(P("section", "ctx", None), P("section", "ctx", None), P("section", "ctx", None)),
        check_vma=False,
    )
```

```python
import functools

import jax
import jax.numpy as jnp
from jax import lax
from jax.experimental import pallas as pl
from jax.experimental.pallas import tpu as pltpu
from jax.sharding import PartitionSpec as P

HOPS = 2
ORDERS = ((2, 1), (1, 2))
TABLE_ROWS = 16
LAST_ROW = 0
COUNT_ROW = 8
FACT_ROWS = 8
NONE, FEW_KEYS, FEW_QUERIES, ALL = range(4)
BACK_STRIDE = 4
EARLY_HEADS = 4
LOG2_E = 1.4426950408889634
MASKED = -1e30

F32 = jnp.float32
BF16 = jnp.bfloat16


def from_behind(block, axis, distance):
    devices = range(lax.axis_size(axis))
    route = [((i - distance) % len(devices), i) for i in devices]
    return lax.ppermute(block, axis, route)


def full_routes(sections, shards, by, parity):
    route = {}
    for at in range(0, sections, 2):
        there, back = at + parity, at + 1 - parity
        for c in range(shards - by):
            route[there, c] = (there, c + by)
        free = set(range(shards))
        for last in range(shards - by, shards):
            first = last - shards + by
            way = [(there, last)] + [(back, c) for c in range(last, by - 1, -BACK_STRIDE)] + [(back, first), (there, first)]
            free -= {c for section, c in way if section == back}
            route.update(zip(way, way[1:]))
        for lane in range(BACK_STRIDE):
            rest = [c for c in sorted(free) if c % BACK_STRIDE == lane]
            pairs = [(c, c + 1) for c in rest if c + 1 in free] if by > 1 else []
            if by == 1:
                pairs = list(zip(rest[0::2], rest[1::2])) if len(rest) % 2 == 0 else []
                if not pairs:
                    route.update({(back, c): (back, rest[k - len(rest) + 1]) for k, c in enumerate(rest)})
            for c, d in pairs:
                route.update({(back, c): (back, d), (back, d): (back, c)})
    full = sections * shards
    whole = len(route) == full and len(set(route.values())) == full and all(a != b for a, b in route.items())
    return [(a * shards + c, b * shards + d) for (a, c), (b, d) in sorted(route.items())] if whole else None


def routes_behind(sections, shards, hop, parity):
    whole = sections % 2 == 0 and shards >= 4 * BACK_STRIDE
    route = full_routes(sections, shards, hop, parity) if whole else None
    if route is None:
        route = [(s * shards + c, s * shards + c + hop) for s in range(parity, sections, 2) for c in range(shards - hop)]
    return route


def returned(sums, order):
    sections, shards = lax.axis_size("section"), lax.axis_size("ctx")
    hop_of = lambda section: order[section % 2]
    route = {(s, c): (s, c - hop_of(s)) for s in range(sections) for c in range(hop_of(s), shards)}
    idle = [(s, c) for s in range(sections) for c in range(shards - hop_of(s), shards)]
    for s in range(sections):
        for c in range(hop_of(s)):
            route[s, c] = min(idle, key=lambda there: ((there[1] - c) % 2, there))
            idle.remove(route[s, c])
    return lax.ppermute(sums, ("section", "ctx"), [(s * shards + c, t * shards + d) for (s, c), (t, d) in route.items()])


def dot_nt(a, b):
    return lax.dot_general(a, b, (((1,), (1,)), ((), ())), preferred_element_type=F32)


def dot_nn(a, b):
    return lax.dot_general(a, b, (((1,), (0,)), ((), ())), preferred_element_type=F32)


def pack_kernel(keys, values, docs, packed, docs_row, docs_here, sems):
    rows, width = keys.shape[1:]
    copies = [
        pltpu.make_async_copy(docs, docs_here, sems.at[0]),
        pltpu.make_async_copy(keys.at[0], packed.at[0:rows, :], sems.at[1]),
        pltpu.make_async_copy(values.at[0], packed.at[rows : 2 * rows, :], sems.at[2]),
    ]
    for copy in copies:
        copy.start()
    copies[0].wait()
    numbers = docs_here[...]
    last = jnp.max(numbers, axis=1, keepdims=True)
    last_count = jnp.sum((numbers == last).astype(F32), axis=1, keepdims=True)
    row_at = lax.broadcasted_iota(jnp.int32, (TABLE_ROWS, width), 0)
    table = jnp.where(row_at == COUNT_ROW, last_count, last.astype(F32) + 1)
    packed[2 * rows : 2 * rows + TABLE_ROWS, :] = table.astype(BF16)
    docs_row[...] = jnp.broadcast_to(numbers.astype(F32) + 1, docs_row.shape)
    for copy in copies[1:]:
        copy.wait()


def column_of(row, width):
    rows = row.shape[1]
    column = jnp.transpose(jnp.broadcast_to(row, (width, rows)))
    return jnp.concatenate([column] * (rows // width), axis=1)


def block_grads(queries, grads, log_sums, delta_of, block, bias, score_grads, weights_low, sums, first_key, query_rows, chosen=None):
    rows = queries.shape[1]
    width = block.shape[1]
    chosen = range(log_sums.shape[1]) if chosen is None else chosen
    scale = float(width) ** -0.5
    beside = rows // query_rows
    key_rows = slice(first_key, rows)
    side = lambda pieces: pieces[0] if len(pieces) == 1 else jnp.concatenate(pieces, axis=1)
    under = lambda pieces: pieces[0] if len(pieces) == 1 else jnp.concatenate(pieces, axis=0)
    part = lambda ref, head: ref[0, 0:query_rows, head * width : (head + 1) * width]
    columns = lambda head: slice(head * rows, head * rows + query_rows)
    masked = side([bias[key_rows, 0:query_rows]] * beside)
    for head in chosen[::beside]:
        group = range(head, head + beside)
        g = under([part(grads, h) for h in group])
        delta = side([delta_of(h, part(grads, h))[:, 0:query_rows] for h in group])
        lse = side([log_sums[0, h : h + 1, 0:query_rows] for h in group]) * LOG2_E
        scores = dot_nt(block[key_rows, :], under([part(queries, h) for h in group]))
        weights = jnp.exp2(scores * (scale * LOG2_E) - lse + masked)
        weight_grads = dot_nt(block[rows + first_key : 2 * rows, :], g)
        low = (weights * (weight_grads - delta)).astype(BF16)
        weights = weights.astype(BF16)
        for at, h in enumerate(group):
            here = slice(at * query_rows, (at + 1) * query_rows)
            score_grads[key_rows, columns(h)] = low[:, here]
            weights_low[key_rows, columns(h)] = weights[:, here]
    straight = slice(chosen[0] * rows, (chosen[-1] + 1) * rows)
    everything = lambda ref: ref[key_rows, straight] if beside == 1 else side([ref[key_rows, columns(h)] for h in chosen])
    stacked = lambda ref: under([part(ref, h) for h in chosen])
    sums[key_rows, 0:width] = (dot_nn(everything(score_grads), stacked(queries)) * scale).astype(sums.dtype)
    sums[key_rows, width : 2 * width] = dot_nn(everything(weights_low), stacked(grads)).astype(sums.dtype)


def own_bias(docs_row, width, bias):
    rows = bias.shape[0]
    docs = docs_row[0:1, :]
    key_at = lax.broadcasted_iota(jnp.int32, (rows, rows), 0)
    query_at = lax.broadcasted_iota(jnp.int32, (rows, rows), 1)
    bias[...] = jnp.where((column_of(docs, width) == docs) & (key_at <= query_at), 0.0, MASKED)


def own_kernel(chosen, queries, attn_out, grads, log_sums, docs_row, block, score_grads, sums, deltas, block_again, bias, weights_low):
    rows = queries.shape[1]
    heads = log_sums.shape[1]
    width = block.shape[1]
    block_again[...] = block[...]
    docs = docs_row[0:1, :]
    first_count = jnp.sum((docs == docs[:, 0:1]).astype(F32), axis=1, keepdims=True)
    deltas[heads:, :] = jnp.broadcast_to(first_count, (FACT_ROWS, rows))
    own_bias(docs_row, width, bias)
    one = jnp.ones((8, width), BF16)
    for head in range(heads):
        part = slice(head * width, (head + 1) * width)
        product = grads[0, :, part].astype(F32) * attn_out[0, :, part].astype(F32)
        high = product.astype(BF16)
        low = (product - high.astype(F32)).astype(BF16)
        deltas[head : head + 1, :] = (dot_nt(one, high) + dot_nt(one, low))[0:1]
    delta_of = lambda head, g: deltas[head : head + 1, :]
    block_grads(queries, grads, log_sums, delta_of, block, bias, score_grads, weights_low, sums, 0, rows, chosen)


def rest_kernel(chosen, queries, grads, log_sums, docs_row, deltas, block, before, first_grads, score_grads, sums, bias, weights_low):
    own_bias(docs_row, block.shape[1], bias)
    delta_of = lambda head, g: deltas[head : head + 1, :]
    block_grads(queries, grads, log_sums, delta_of, block, bias, score_grads, weights_low, sums, 0, queries.shape[1], chosen)


def hop_kernel(hop, parity, queries, grads, log_sums, docs_row, deltas, block, before, *refs):
    score_grads, sums, bias, weights_low = refs[-4:]

    def reachable():
        rows = queries.shape[1]
        half = rows // 2
        docs = docs_row[0:1, :]
        table = block[2 * rows : 2 * rows + TABLE_ROWS, :].astype(F32)
        same = (table[LAST_ROW : LAST_ROW + 1, 0:1] == docs[:, 0:1]) & (lax.axis_index("ctx") >= hop)
        key_count = jnp.where(same, table[COUNT_ROW : COUNT_ROW + 1, 0:1], 0.0)
        query_count = deltas[log_sums.shape[1] : log_sums.shape[1] + 1, 0:1]
        key_at = lax.broadcasted_iota(jnp.int32, (rows, rows), 0).astype(F32)
        bias[...] = jnp.where((key_at >= rows - key_count) & (docs == docs[:, 0:1]), 0.0, MASKED)
        some = jnp.where(query_count <= half, FEW_QUERIES, ALL)
        mode = jnp.where(key_count == 0, NONE, jnp.where(key_count <= half, FEW_KEYS, some))[0, 0]
        delta_of = lambda head, g: deltas[head : head + 1, :]
        work = functools.partial(block_grads, queries, grads, log_sums, delta_of, block, bias, score_grads, weights_low, sums)

        @pl.when(mode == NONE)
        def _():
            score_grads[...] = jnp.zeros_like(score_grads)
            sums[...] = jnp.zeros_like(sums)

        @pl.when(mode == FEW_KEYS)
        def _():
            score_grads[0:half, :] = jnp.zeros((half, score_grads.shape[1]), BF16)
            sums[0:half, :] = jnp.zeros((half, sums.shape[1]), BF16)
            work(half, rows)

        @pl.when(mode == FEW_QUERIES)
        def _():
            for head in range(score_grads.shape[1] // rows):
                score_grads[:, head * rows + half : (head + 1) * rows] = jnp.zeros((rows, rows - half), BF16)
            work(0, half)

        if hop < HOPS:

            @pl.when(mode == ALL)
            def _():
                work(0, rows)

    pl.when(lax.axis_index("section") % 2 == parity)(reachable)


def pick(candidates, block):
    for parity, candidate in enumerate(candidates):

        @pl.when(lax.axis_index("section") % 2 == parity)
        def _():
            block[...] = candidate[...]


def query_kernel(own, own_grads, first_grads, second_grads, first_even, first_odd, second_even, second_odd, grad_queries, first, second):
    pick((first_even, first_odd), first)
    pick((second_even, second_odd), second)
    rows = own_grads.shape[0]
    heads = own_grads.shape[1] // rows
    width = own.shape[1]
    scale = float(width) ** -0.5
    turned = [jnp.transpose(block[0:rows, :].astype(F32)).astype(BF16) for block in (own, first, second)]
    for head in range(heads):
        columns = slice(head * rows, (head + 1) * rows)
        total = dot_nn(turned[0], own_grads[:, columns]) + dot_nn(turned[1], first_grads[:, columns]) + dot_nn(turned[2], second_grads[:, columns])
        grad_queries[0, :, head * width : (head + 1) * width] = jnp.transpose(total * scale).astype(BF16)


def reached(order, shards):
    hop = jnp.where(lax.axis_index("section") % 2 == 0, *order)
    return lax.axis_index("ctx") + hop < shards


def fold_kernel(shards, own_sums, rest_sums, first_sums, total):
    total[...] = own_sums[...] + rest_sums[...]

    @pl.when(reached(ORDERS[0], shards))
    def _():
        total[...] += first_sums[...].astype(F32)


def add_kernel(shards, folded, second_sums, grad_keys, grad_values, low, sems):
    rows, width = grad_keys.shape[1:]
    there = reached(ORDERS[1], shards).astype(F32)
    copies = []
    for at, target in enumerate((grad_keys, grad_values)):
        half = slice(at * width, (at + 1) * width)
        low[at] = (folded[:, half] + second_sums[:, half].astype(F32) * there).astype(BF16)
        copies.append(pltpu.make_async_copy(low.at[at], target.at[0], sems.at[at]))
        copies[-1].start()
    for copy in copies:
        copy.wait()


def call(kernel, name, outs, args, flops=0, scratch=(), from_hbm=0, kept=(), limit=8, to_hbm=False):
    args = [pltpu.with_memory_space_constraint(a, pltpu.HBM) for a in args[:from_hbm]] + list(args[from_hbm:])
    moved = sum(a.size * a.dtype.itemsize for a in args)
    vmem = lambda count: [pl.BlockSpec(memory_space=pltpu.VMEM)] * count
    return pl.pallas_call(
        kernel,
        out_shape=outs,
        in_specs=[pl.BlockSpec(memory_space=pltpu.HBM)] * from_hbm + vmem(len(args) - from_hbm + len(kept)),
        out_specs=tuple([pl.BlockSpec(memory_space=pltpu.HBM)] * len(outs) if to_hbm else vmem(len(outs))),
        scratch_shapes=list(scratch),
        input_output_aliases={len(args) + i: i for i in range(len(kept))},
        compiler_params=pltpu.CompilerParams(vmem_limit_bytes=limit * 1024 * 1024),
        cost_estimate=pl.CostEstimate(flops=flops, bytes_accessed=moved, transcendentals=0),
        name=name,
    )(*args, *kept)


def per_device(queries, keys, values, attn_out, log_sums, grad_held, doc_ids):
    rows, width = keys.shape[1:]
    heads = log_sums.shape[1]
    shape = jax.ShapeDtypeStruct
    flops = 2 * heads * rows * rows * width
    score_grads = shape((rows, heads * rows), BF16)
    scratch = [pltpu.VMEM((rows, rows), F32), pltpu.VMEM((rows, heads * rows), BF16)]
    sums = lambda dtype: shape((rows, 2 * width), dtype)

    grads = from_behind(grad_held, "section", -1)
    own, docs_row = call(
        pack_kernel,
        "pack",
        (shape((2 * rows + TABLE_ROWS, width), BF16), shape((8, rows), F32)),
        (keys, values, doc_ids.reshape(1, rows)),
        40 * flops,
        [pltpu.VMEM((1, rows), jnp.int32), pltpu.SemaphoreType.DMA((3,))],
        3,
    )
    sections, shards = lax.axis_size("section"), lax.axis_size("ctx")
    behind = lambda block, order: [
        lax.ppermute(block, ("section", "ctx"), routes_behind(sections, shards, hop, parity)) for parity, hop in enumerate(order)
    ]
    first_order, second_order = ORDERS
    first = behind(own, first_order)
    early = range(EARLY_HEADS * heads // 8)
    late = range(len(early), heads)
    own_grads, own_sums, deltas, own_again = call(
        functools.partial(own_kernel, early),
        "own_block",
        (score_grads, sums(F32), shape((heads + FACT_ROWS, rows), F32), shape(own.shape, BF16)),
        (queries, attn_out, grads, log_sums, docs_row, own),
        4 * flops,
        scratch,
    )
    second = behind(own_again, second_order)

    def block_of(name, order, before, candidates):
        kept = ()
        for parity, (hop, block) in enumerate(zip(order, candidates)):
            args = (queries, grads, log_sums, docs_row, deltas, block, before)
            kept = call(functools.partial(hop_kernel, hop, parity), name, (score_grads, sums(BF16)), args, 4 * flops, scratch, 0, kept)
        return kept

    first_grads, first_sums = block_of("first_block", first_order, own_sums, first)
    first_back = returned(first_sums, first_order)
    second_grads, second_sums = block_of("second_block", second_order, first_sums, second)
    second_back = returned(second_sums, second_order)
    own_grads, rest_sums = call(
        functools.partial(rest_kernel, late),
        "own_rest",
        (score_grads, sums(F32)),
        (queries, grads, log_sums, docs_row, deltas, own, second_sums),
        2 * flops,
        scratch,
        0,
        (own_grads,),
    )
    (grad_queries,) = call(
        query_kernel,
        "query_grads",
        (shape(queries.shape, BF16),),
        (own, own_grads, first_grads, second_grads, *first, *second),
        3 * flops,
        [pltpu.VMEM(own.shape, BF16)] * 2,
    )
    (folded,) = call(functools.partial(fold_kernel, shards), "fold", (sums(F32),), (own_sums, rest_sums, first_back))
    grad_keys, grad_values = call(
        functools.partial(add_kernel, shards),
        "add",
        (shape(keys.shape, BF16), shape(values.shape, BF16)),
        (folded, second_back),
        0,
        [pltpu.VMEM((2, rows, width), BF16), pltpu.SemaphoreType.DMA((2,))],
        to_hbm=True,
    )
    return grad_queries, grad_keys, grad_values


def solution(mesh):
    placed = (
        P("section", "ctx", None),
        P("section", "ctx", None),
        P("section", "ctx", None),
        P("section", "ctx", None),
        P("section", None, "ctx"),
        P("section", "ctx", None),
        P("ctx"),
    )
    return jax.shard_map(
        per_device,
        mesh=mesh,
        in_specs=placed,
        out_specs=(P("section", "ctx", None), P("section", "ctx", None), P("section", "ctx", None)),
        check_vma=False,
    )
```

```python
import functools

import jax
import jax.numpy as jnp
from jax import lax
from jax.experimental import pallas as pl
from jax.experimental.pallas import tpu as pltpu
from jax.sharding import PartitionSpec as P

HOPS = 2
ORDERS = ((2, 1), (1, 2))
TABLE_ROWS = 16
LAST_ROW = 0
COUNT_ROW = 8
FACT_ROWS = 8
NONE, FEW_KEYS, FEW_QUERIES, ALL = range(4)
BACK_STRIDE = 4
EARLY_HEADS = 4
LOG2_E = 1.4426950408889634
MASKED = -1e30

F32 = jnp.float32
BF16 = jnp.bfloat16


def from_behind(block, axis, distance):
    devices = range(lax.axis_size(axis))
    route = [((i - distance) % len(devices), i) for i in devices]
    return lax.ppermute(block, axis, route)


def full_routes(sections, shards, by, parity):
    route = {}
    for at in range(0, sections, 2):
        there, back = at + parity, at + 1 - parity
        for c in range(shards - by):
            route[there, c] = (there, c + by)
        free = set(range(shards))
        for last in range(shards - by, shards):
            first = last - shards + by
            way = [(there, last)] + [(back, c) for c in range(last, by - 1, -BACK_STRIDE)] + [(back, first), (there, first)]
            free -= {c for section, c in way if section == back}
            route.update(zip(way, way[1:]))
        for lane in range(BACK_STRIDE):
            rest = [c for c in sorted(free) if c % BACK_STRIDE == lane]
            pairs = [(c, c + 1) for c in rest if c + 1 in free] if by > 1 else []
            if by == 1:
                pairs = list(zip(rest[0::2], rest[1::2])) if len(rest) % 2 == 0 else []
                if not pairs:
                    route.update({(back, c): (back, rest[k - len(rest) + 1]) for k, c in enumerate(rest)})
            for c, d in pairs:
                route.update({(back, c): (back, d), (back, d): (back, c)})
    full = sections * shards
    whole = len(route) == full and len(set(route.values())) == full and all(a != b for a, b in route.items())
    return [(a * shards + c, b * shards + d) for (a, c), (b, d) in sorted(route.items())] if whole else None


def routes_behind(sections, shards, hop, parity):
    whole = sections % 2 == 0 and shards >= 4 * BACK_STRIDE
    route = full_routes(sections, shards, hop, parity) if whole else None
    if route is None:
        route = [(s * shards + c, s * shards + c + hop) for s in range(parity, sections, 2) for c in range(shards - hop)]
    return route


def returned(sums, order):
    sections, shards = lax.axis_size("section"), lax.axis_size("ctx")
    hop_of = lambda section: order[section % 2]
    route = {(s, c): (s, c - hop_of(s)) for s in range(sections) for c in range(hop_of(s), shards)}
    idle = [(s, c) for s in range(sections) for c in range(shards - hop_of(s), shards)]
    for s in range(sections):
        for c in range(hop_of(s)):
            route[s, c] = min(idle, key=lambda there: ((there[1] - c) % 2, abs(there[0] - s)))
            idle.remove(route[s, c])
    return lax.ppermute(sums, ("section", "ctx"), [(s * shards + c, t * shards + d) for (s, c), (t, d) in route.items()])


def dot_nt(a, b):
    return lax.dot_general(a, b, (((1,), (1,)), ((), ())), preferred_element_type=F32)


def dot_nn(a, b):
    return lax.dot_general(a, b, (((1,), (0,)), ((), ())), preferred_element_type=F32)


def pack_kernel(keys, values, docs, packed, docs_row, docs_here, sems):
    rows, width = keys.shape[1:]
    copies = [
        pltpu.make_async_copy(docs, docs_here, sems.at[0]),
        pltpu.make_async_copy(keys.at[0], packed.at[0:rows, :], sems.at[1]),
        pltpu.make_async_copy(values.at[0], packed.at[rows : 2 * rows, :], sems.at[2]),
    ]
    for copy in copies:
        copy.start()
    copies[0].wait()
    numbers = docs_here[...]
    last = jnp.max(numbers, axis=1, keepdims=True)
    last_count = jnp.sum((numbers == last).astype(F32), axis=1, keepdims=True)
    row_at = lax.broadcasted_iota(jnp.int32, (TABLE_ROWS, width), 0)
    table = jnp.where(row_at == COUNT_ROW, last_count, last.astype(F32) + 1)
    packed[2 * rows : 2 * rows + TABLE_ROWS, :] = table.astype(BF16)
    docs_row[...] = jnp.broadcast_to(numbers.astype(F32) + 1, docs_row.shape)
    for copy in copies[1:]:
        copy.wait()


def column_of(row, width):
    rows = row.shape[1]
    column = jnp.transpose(jnp.broadcast_to(row, (width, rows)))
    return jnp.concatenate([column] * (rows // width), axis=1)


def block_grads(queries, grads, log_sums, delta_of, block, bias, score_grads, weights_low, sums, first_key, query_rows, chosen=None):
    rows = queries.shape[1]
    width = block.shape[1]
    chosen = range(log_sums.shape[1]) if chosen is None else chosen
    scale = float(width) ** -0.5
    beside = rows // query_rows
    key_rows = slice(first_key, rows)
    side = lambda pieces: pieces[0] if len(pieces) == 1 else jnp.concatenate(pieces, axis=1)
    under = lambda pieces: pieces[0] if len(pieces) == 1 else jnp.concatenate(pieces, axis=0)
    part = lambda ref, head: ref[0, 0:query_rows, head * width : (head + 1) * width]
    columns = lambda head: slice(head * rows, head * rows + query_rows)
    masked = side([bias[key_rows, 0:query_rows]] * beside)
    for head in chosen[::beside]:
        group = range(head, head + beside)
        g = under([part(grads, h) for h in group])
        delta = side([delta_of(h, part(grads, h))[:, 0:query_rows] for h in group])
        lse = side([log_sums[0, h : h + 1, 0:query_rows] for h in group]) * LOG2_E
        scores = dot_nt(block[key_rows, :], under([part(queries, h) for h in group]))
        weights = jnp.exp2(scores * (scale * LOG2_E) - lse + masked)
        weight_grads = dot_nt(block[rows + first_key : 2 * rows, :], g)
        low = (weights * (weight_grads - delta)).astype(BF16)
        weights = weights.astype(BF16)
        for at, h in enumerate(group):
            here = slice(at * query_rows, (at + 1) * query_rows)
            score_grads[key_rows, columns(h)] = low[:, here]
            weights_low[key_rows, columns(h)] = weights[:, here]
    straight = slice(chosen[0] * rows, (chosen[-1] + 1) * rows)
    everything = lambda ref: ref[key_rows, straight] if beside == 1 else side([ref[key_rows, columns(h)] for h in chosen])
    stacked = lambda ref: under([part(ref, h) for h in chosen])
    sums[key_rows, 0:width] = (dot_nn(everything(score_grads), stacked(queries)) * scale).astype(sums.dtype)
    sums[key_rows, width : 2 * width] = dot_nn(everything(weights_low), stacked(grads)).astype(sums.dtype)


def own_bias(docs_row, width, bias):
    rows = bias.shape[0]
    docs = docs_row[0:1, :]
    key_at = lax.broadcasted_iota(jnp.int32, (rows, rows), 0)
    query_at = lax.broadcasted_iota(jnp.int32, (rows, rows), 1)
    bias[...] = jnp.where((column_of(docs, width) == docs) & (key_at <= query_at), 0.0, MASKED)


def own_kernel(chosen, queries, attn_out, grads, log_sums, docs_row, block, score_grads, sums, deltas, block_again, bias, weights_low):
    rows = queries.shape[1]
    heads = log_sums.shape[1]
    width = block.shape[1]
    block_again[...] = block[...]
    docs = docs_row[0:1, :]
    first_count = jnp.sum((docs == docs[:, 0:1]).astype(F32), axis=1, keepdims=True)
    deltas[heads:, :] = jnp.broadcast_to(first_count, (FACT_ROWS, rows))
    own_bias(docs_row, width, bias)
    one = jnp.ones((8, width), BF16)
    for head in range(heads):
        part = slice(head * width, (head + 1) * width)
        product = grads[0, :, part].astype(F32) * attn_out[0, :, part].astype(F32)
        high = product.astype(BF16)
        low = (product - high.astype(F32)).astype(BF16)
        deltas[head : head + 1, :] = (dot_nt(one, high) + dot_nt(one, low))[0:1]
    delta_of = lambda head, g: deltas[head : head + 1, :]
    block_grads(queries, grads, log_sums, delta_of, block, bias, score_grads, weights_low, sums, 0, rows, chosen)


def rest_kernel(chosen, queries, grads, log_sums, docs_row, deltas, block, before, first_grads, score_grads, sums, bias, weights_low):
    own_bias(docs_row, block.shape[1], bias)
    delta_of = lambda head, g: deltas[head : head + 1, :]
    block_grads(queries, grads, log_sums, delta_of, block, bias, score_grads, weights_low, sums, 0, queries.shape[1], chosen)


def hop_kernel(hop, parity, queries, grads, log_sums, docs_row, deltas, block, before, *refs):
    score_grads, sums, bias, weights_low = refs[-4:]

    def reachable():
        rows = queries.shape[1]
        half = rows // 2
        docs = docs_row[0:1, :]
        table = block[2 * rows : 2 * rows + TABLE_ROWS, :].astype(F32)
        same = (table[LAST_ROW : LAST_ROW + 1, 0:1] == docs[:, 0:1]) & (lax.axis_index("ctx") >= hop)
        key_count = jnp.where(same, table[COUNT_ROW : COUNT_ROW + 1, 0:1], 0.0)
        query_count = deltas[log_sums.shape[1] : log_sums.shape[1] + 1, 0:1]
        key_at = lax.broadcasted_iota(jnp.int32, (rows, rows), 0).astype(F32)
        bias[...] = jnp.where((key_at >= rows - key_count) & (docs == docs[:, 0:1]), 0.0, MASKED)
        some = jnp.where(query_count <= half, FEW_QUERIES, ALL)
        mode = jnp.where(key_count == 0, NONE, jnp.where(key_count <= half, FEW_KEYS, some))[0, 0]
        delta_of = lambda head, g: deltas[head : head + 1, :]
        work = functools.partial(block_grads, queries, grads, log_sums, delta_of, block, bias, score_grads, weights_low, sums)

        @pl.when(mode == NONE)
        def _():
            score_grads[...] = jnp.zeros_like(score_grads)
            sums[...] = jnp.zeros_like(sums)

        @pl.when(mode == FEW_KEYS)
        def _():
            score_grads[0:half, :] = jnp.zeros((half, score_grads.shape[1]), BF16)
            sums[0:half, :] = jnp.zeros((half, sums.shape[1]), BF16)
            work(half, rows)

        @pl.when(mode == FEW_QUERIES)
        def _():
            for head in range(score_grads.shape[1] // rows):
                score_grads[:, head * rows + half : (head + 1) * rows] = jnp.zeros((rows, rows - half), BF16)
            work(0, half)

        if hop < HOPS:

            @pl.when(mode == ALL)
            def _():
                work(0, rows)

    pl.when(lax.axis_index("section") % 2 == parity)(reachable)


def pick(candidates, block):
    for parity, candidate in enumerate(candidates):

        @pl.when(lax.axis_index("section") % 2 == parity)
        def _():
            block[...] = candidate[...]


def query_kernel(own, own_grads, first_grads, second_grads, first_even, first_odd, second_even, second_odd, grad_queries, first, second):
    pick((first_even, first_odd), first)
    pick((second_even, second_odd), second)
    rows = own_grads.shape[0]
    heads = own_grads.shape[1] // rows
    width = own.shape[1]
    scale = float(width) ** -0.5
    turned = [jnp.transpose(block[0:rows, :].astype(F32)).astype(BF16) for block in (own, first, second)]
    for head in range(heads):
        columns = slice(head * rows, (head + 1) * rows)
        total = dot_nn(turned[0], own_grads[:, columns]) + dot_nn(turned[1], first_grads[:, columns]) + dot_nn(turned[2], second_grads[:, columns])
        grad_queries[0, :, head * width : (head + 1) * width] = jnp.transpose(total * scale).astype(BF16)


def reached(order, shards):
    hop = jnp.where(lax.axis_index("section") % 2 == 0, *order)
    return lax.axis_index("ctx") + hop < shards


def fold_kernel(shards, own_sums, rest_sums, first_sums, total):
    total[...] = own_sums[...] + rest_sums[...]

    @pl.when(reached(ORDERS[0], shards))
    def _():
        total[...] += first_sums[...].astype(F32)


def add_kernel(shards, folded, second_sums, grad_keys, grad_values, low, sems):
    rows, width = grad_keys.shape[1:]
    there = reached(ORDERS[1], shards).astype(F32)
    copies = []
    for at, target in enumerate((grad_keys, grad_values)):
        half = slice(at * width, (at + 1) * width)
        low[at] = (folded[:, half] + second_sums[:, half].astype(F32) * there).astype(BF16)
        copies.append(pltpu.make_async_copy(low.at[at], target.at[0], sems.at[at]))
        copies[-1].start()
    for copy in copies:
        copy.wait()


def call(kernel, name, outs, args, flops=0, scratch=(), from_hbm=0, kept=(), limit=8, to_hbm=False):
    args = [pltpu.with_memory_space_constraint(a, pltpu.HBM) for a in args[:from_hbm]] + list(args[from_hbm:])
    moved = sum(a.size * a.dtype.itemsize for a in args)
    vmem = lambda count: [pl.BlockSpec(memory_space=pltpu.VMEM)] * count
    return pl.pallas_call(
        kernel,
        out_shape=outs,
        in_specs=[pl.BlockSpec(memory_space=pltpu.HBM)] * from_hbm + vmem(len(args) - from_hbm + len(kept)),
        out_specs=tuple([pl.BlockSpec(memory_space=pltpu.HBM)] * len(outs) if to_hbm else vmem(len(outs))),
        scratch_shapes=list(scratch),
        input_output_aliases={len(args) + i: i for i in range(len(kept))},
        compiler_params=pltpu.CompilerParams(vmem_limit_bytes=limit * 1024 * 1024),
        cost_estimate=pl.CostEstimate(flops=flops, bytes_accessed=moved, transcendentals=0),
        name=name,
    )(*args, *kept)


def per_device(queries, keys, values, attn_out, log_sums, grad_held, doc_ids):
    rows, width = keys.shape[1:]
    heads = log_sums.shape[1]
    shape = jax.ShapeDtypeStruct
    flops = 2 * heads * rows * rows * width
    score_grads = shape((rows, heads * rows), BF16)
    scratch = [pltpu.VMEM((rows, rows), F32), pltpu.VMEM((rows, heads * rows), BF16)]
    sums = lambda dtype: shape((rows, 2 * width), dtype)

    grads = from_behind(grad_held, "section", -1)
    own, docs_row = call(
        pack_kernel,
        "pack",
        (shape((2 * rows + TABLE_ROWS, width), BF16), shape((8, rows), F32)),
        (keys, values, doc_ids.reshape(1, rows)),
        40 * flops,
        [pltpu.VMEM((1, rows), jnp.int32), pltpu.SemaphoreType.DMA((3,))],
        3,
    )
    sections, shards = lax.axis_size("section"), lax.axis_size("ctx")
    behind = lambda block, order: [
        lax.ppermute(block, ("section", "ctx"), routes_behind(sections, shards, hop, parity)) for parity, hop in enumerate(order)
    ]
    first_order, second_order = ORDERS
    first = behind(own, first_order)
    early = range(EARLY_HEADS * heads // 8)
    late = range(len(early), heads)
    own_grads, own_sums, deltas, own_again = call(
        functools.partial(own_kernel, early),
        "own_block",
        (score_grads, sums(F32), shape((heads + FACT_ROWS, rows), F32), shape(own.shape, BF16)),
        (queries, attn_out, grads, log_sums, docs_row, own),
        4 * flops,
        scratch,
    )
    sent = lambda block, parity: lax.ppermute(block, ("section", "ctx"), routes_behind(sections, shards, second_order[parity], parity))
    second = [sent(own_again, 0), sent(own, 1)]

    def block_of(name, order, before, candidates):
        kept = ()
        for parity, (hop, block) in enumerate(zip(order, candidates)):
            args = (queries, grads, log_sums, docs_row, deltas, block, before)
            kept = call(functools.partial(hop_kernel, hop, parity), name, (score_grads, sums(BF16)), args, 4 * flops, scratch, 0, kept)
        return kept

    first_grads, first_sums = block_of("first_block", first_order, own_sums, first)
    first_back = returned(first_sums, first_order)
    second_grads, second_sums = block_of("second_block", second_order, first_sums, second)
    second_back = returned(second_sums, second_order)
    own_grads, rest_sums = call(
        functools.partial(rest_kernel, late),
        "own_rest",
        (score_grads, sums(F32)),
        (queries, grads, log_sums, docs_row, deltas, own, second_sums),
        2 * flops,
        scratch,
        0,
        (own_grads,),
    )
    (grad_queries,) = call(
        query_kernel,
        "query_grads",
        (shape(queries.shape, BF16),),
        (own, own_grads, first_grads, second_grads, *first, *second),
        3 * flops,
        [pltpu.VMEM(own.shape, BF16)] * 2,
    )
    (folded,) = call(functools.partial(fold_kernel, shards), "fold", (sums(F32),), (own_sums, rest_sums, first_back))
    grad_keys, grad_values = call(
        functools.partial(add_kernel, shards),
        "add",
        (shape(keys.shape, BF16), shape(values.shape, BF16)),
        (folded, second_back),
        0,
        [pltpu.VMEM((2, rows, width), BF16), pltpu.SemaphoreType.DMA((2,))],
        to_hbm=True,
    )
    return grad_queries, grad_keys, grad_values


def solution(mesh):
    placed = (
        P("section", "ctx", None),
        P("section", "ctx", None),
        P("section", "ctx", None),
        P("section", "ctx", None),
        P("section", None, "ctx"),
        P("section", "ctx", None),
        P("ctx"),
    )
    return jax.shard_map(
        per_device,
        mesh=mesh,
        in_specs=placed,
        out_specs=(P("section", "ctx", None), P("section", "ctx", None), P("section", "ctx", None)),
        check_vma=False,
    )
```
